512 devices in a mesh: dp: 8 (over x, z_lo), ctx: 64 (over z_hi, y, core).
Axes of the slice: x: 4, y: 8, z: 8 (z_hi: 4, z_lo: 2; z = z_hi * 2 + z_lo), core: 2. Of those that a mesh axis runs over, the one named last changes fastest.
Arguments:
- level_input: bfloat16 [8, 65536, 256], P('dp', 'ctx'), may hold values from -6 to 6
- saved_forward: bfloat16 [3, 8, 65536, 256], P(None, 'dp', 'ctx'), may hold values from -6 to 6
- saved_reverse: bfloat16 [3, 8, 65536, 256], P(None, 'dp', 'ctx'), may hold values from -6 to 6
- filters: float32 [2, 2, 2, 256], replicated, may hold values from -2.5 to 2.5
- mixing: float32 [2, 5, 256], replicated, may hold values from -3 to 3
- cotangent: bfloat16 [8, 65536, 256], P('dp', 'ctx'), may hold values from -33 to 33
Outputs:
- grad_input: bfloat16 [8, 65536, 256], P('dp', 'ctx')
- grad_filters: float32 [2, 2, 2, 256], replicated
- grad_mixing: float32 [2, 5, 256], replicated
The draws below stay inside these ranges and needn't reach their ends.
All inputs are finite; a program needn't handle non-finite values.
Results may differ from the reference program's by a relative error of at most 0.0065.
Values may be sent and summed in bfloat16 or wider, within the bound.
No kernel may reach another device: no remote copies, remote signals or barrier semaphores. Data moves between devices by JAX's collectives and lax.ppermute only.
A program may use at most 64 MiB of HBM per device.

```python
import math
import jax
import jax.numpy as jnp
from jax import lax

C = 256
LEVELS = 4
BASE = 128
SEQS = 8
LENGTH = 65536


def draw_cotangent(key, part):
    key = jax.random.fold_in(key, 7)
    first = jax.random.fold_in(key, 0)
    shape = (SEQS, LENGTH, C)
    where = jnp.arange(LENGTH, dtype=jnp.float32) / (LENGTH - 1)
    ramp = jnp.exp(math.log(3.0) * where)[None, :, None]
    values = jnp.clip(jax.random.normal(first, shape, jnp.float32), -5.0, 5.0)
    return (values * ramp).astype(jnp.bfloat16)


def block_scale(stream_key, shape, cuts, least, high):
    def one(position, blocks):
        draws = jax.random.uniform(jax.random.fold_in(jax.random.fold_in(stream_key, 6), position), (blocks,), jnp.float32, least / len(cuts), high / len(cuts))
        return jnp.repeat(jnp.exp(draws), shape[position] // blocks).reshape((-1,) + (1,) * (len(shape) - position - 1))

    loudness = one(*cuts[0])
    for cut in cuts[1:]:
        loudness = loudness * one(*cut)
    return loudness


def centred(stream_key, dims, width, most, shards=(), held_as=jnp.bfloat16):
    values = width * jax.random.normal(stream_key, dims, jnp.float32)
    if shards:
        values = values * block_scale(stream_key, dims, shards, -0.22, 0.18)
    return jnp.clip(values, -most, most).astype(held_as)


def setup_inputs(seed: int = 0) -> dict:
    seeds = jax.random.split(jax.random.key(seed), 7)
    level_input = centred(seeds[0], (SEQS, LENGTH, C), 1.0, 6.0, ((0, 8), (1, 64)))
    saved_forward = centred(seeds[1], (LEVELS - 1, SEQS, LENGTH, C), 1.0, 6.0, ((1, 8), (2, 64)))
    saved_reverse = centred(seeds[2], (LEVELS - 1, SEQS, LENGTH, C), 1.0, 6.0, ((1, 8), (2, 64)))
    filters = centred(seeds[3], (2, 2, 2, C), 0.7, 2.5, (), jnp.float32)
    mixing = centred(seeds[4], (2, LEVELS + 1, C), 0.6, 3.0, (), jnp.float32)
    cotangent = draw_cotangent(jax.random.fold_in(seeds[6], 71), 0)
    return dict(level_input=level_input, saved_forward=saved_forward, saved_reverse=saved_reverse, filters=filters, mixing=mixing, cotangent=cotangent)


def lag(values, dist):
    return jnp.pad(values, ((0, 0), (dist, 0), (0, 0)))[:, :values.shape[1]]

def lead(values, dist):
    return jnp.pad(values, ((0, 0), (0, dist), (0, 0)))[:, dist:]

def branch_backward(inputs, dy, gains, weights, ahead):
    levels = len(inputs)
    grad = weights[levels] * dy
    filt = jnp.zeros((2, 2, C), jnp.float32)
    mixes = [None] * (levels + 1)
    for level in reversed(range(levels)):
        dist = BASE * 2 ** level
        plain = inputs[level].astype(jnp.float32)
        near = lead(plain, dist) if ahead else lag(plain, dist)
        weight = weights[level]
        s_a = lax.optimization_barrier(jnp.sum(grad * near, axis=(0, 1)))
        s_y = lax.optimization_barrier(jnp.sum(dy * near, axis=(0, 1)))
        t_a = lax.optimization_barrier(jnp.sum(grad * plain, axis=(0, 1)))
        t_y = lax.optimization_barrier(jnp.sum(dy * plain, axis=(0, 1)))
        filt = filt + jnp.stack([jnp.stack([s_a, t_a]), jnp.stack([weight * s_y, weight * t_y])])
        mixes[level] = gains[1, 0] * s_y + gains[1, 1] * t_y
        if level == levels - 1:
            mixes[levels] = gains[0, 0] * s_y + gains[0, 1] * t_y
        shifted = gains[0, 0] * grad + gains[1, 0] * (weight * dy)
        back = lag(shifted, dist) if ahead else lead(shifted, dist)
        grad = gains[0, 1] * grad + gains[1, 1] * (weight * dy) + back
    return (grad, filt, jnp.stack(mixes))

def reference(level_input, saved_forward, saved_reverse, filters, mixing, cotangent):
    dy = cotangent.astype(jnp.float32)
    levels = saved_forward.shape[0] + 1
    inputs_fwd = [level_input] + [saved_forward[i] for i in range(levels - 1)]
    inputs_rev = [level_input] + [saved_reverse[i] for i in range(levels - 1)]
    grad_fwd, filt_fwd, mix_fwd = branch_backward(inputs_fwd, dy, filters[0], mixing[0], False)
    grad_rev, filt_rev, mix_rev = branch_backward(inputs_rev, dy, filters[1], mixing[1], True)
    factor = 1.0 / math.sqrt(cotangent.shape[0] * cotangent.shape[1])
    grad_input = (grad_fwd + grad_rev).astype(jnp.bfloat16)
    grad_filters = jnp.stack([filt_fwd, filt_rev]) * factor
    grad_mixing = jnp.stack([mix_fwd, mix_rev]) * factor
    return (grad_input, grad_filters, grad_mixing)
```

```python
import math

import jax
import jax.numpy as jnp
from jax import lax
from jax.experimental import pallas as pl
from jax.experimental.pallas import tpu as pltpu
from jax.sharding import Mesh
from jax.sharding import PartitionSpec as P

BLOCK = 128
NB = 8
LEVELS = 4
STEP = 16
LANES = 128
TAPS = 16
LAGS = tuple(
    (level, k)
    for level in range(LEVELS)
    for k in range(0, TAPS, 2**level)
)
ROW = {key: i for i, key in enumerate(LAGS)}
ROWS = 32
SUMS = 18
F32 = jnp.float32
DP = ("x", "zl")
CTX = ("zh", "y", "core")


def piece(ref, lead, n, r, cols):
    rows = pl.ds(pl.multiple_of(n * BLOCK + r * STEP, STEP), STEP)
    value = ref[rows, cols] if lead is None else ref[lead, rows, cols]
    return value.astype(F32).reshape(2, STEP // 2, LANES)


def columns(h):
    return pl.ds(h * LANES, LANES)


def add_corr(corr_ref, b, first, saved, dy_ref, delta):
    sign = 1 - 2 * b
    plan = []
    for level in range(LEVELS):
        for n in range(NB):
            for m in range(NB):
                key = (level, delta + sign * (m - n))
                if key in ROW:
                    plan.append((level, n, m, key))
    keys = sorted({p[3] for p in plan})
    slot = {key: i for i, key in enumerate(keys)}
    for h in range(2):
        cols = columns(h)

        def body(r, accs):
            accs = list(accs)
            dys = {m: piece(dy_ref, None, m, r, cols) for m in sorted({p[2] for p in plan})}
            for level in range(LEVELS):
                for n in range(NB):
                    mine = [p for p in plan if p[0] == level and p[1] == n]
                    if not mine:
                        continue
                    value = piece(first, None, n, r, cols) if level == 0 else piece(saved, level - 1, n, r, cols)
                    for _, _, m, key in mine:
                        prod = value * dys[m]
                        accs[slot[key]] = accs[slot[key]] + (prod[0] + prod[1])
            return tuple(accs)

        zero = jnp.zeros((STEP // 2, LANES), F32)
        accs = lax.fori_loop(0, BLOCK // STEP, body, (zero,) * len(keys))
        for key, acc in zip(keys, accs):
            at = (b, pl.ds(ROW[key], 1), cols)
            corr_ref[at] = corr_ref[at] + jnp.sum(acc, axis=0, keepdims=True)


def weights(filters_ref, mixing_ref):
    f = [[filters_ref[:, i, j, :] for j in range(2)] for i in range(2)]
    mix = [mixing_ref[:, i, :] for i in range(LEVELS + 1)]
    now = {0: mix[LEVELS]}
    out = {LEVELS - 1: now}
    for level in reversed(range(LEVELS)):
        d = 2**level
        new = {}
        for k, w in now.items():
            for at, term in ((k, f[0][1] * w), (k + d, f[0][0] * w)):
                new[at] = new[at] + term if at in new else term
        new[0] = new[0] + f[1][1] * mix[level]
        new[d] = new[d] + f[1][0] * mix[level]
        now = new
        out[level - 1] = now
    return f, mix, out


def put_taps(taps_ref, filters_ref, mixing_ref):
    taps = weights(filters_ref, mixing_ref)[2][-1]
    for k in range(TAPS):
        for b in range(2):
            taps_ref[b, k] = jnp.broadcast_to(taps[k][b : b + 1], taps_ref.shape[2:])


def add_filter(taps_ref, terms, r, cols, accs):
    accs = list(accs)
    for b, dy_ref, delta in terms:
        sign = 1 - 2 * b
        for m in range(NB):
            hits = [(n, delta + sign * (m - n)) for n in range(NB) if 0 <= delta + sign * (m - n) < TAPS]
            if not hits:
                continue
            value = piece(dy_ref, None, m, r, cols)
            for n, k in hits:
                accs[n] = accs[n] + value * taps_ref[b, k, :, cols][None]
    return accs


def near_kernel(core_ref, dy_ref, swap_ref, first, fwd, rev, filters_ref, mixing_ref, corr_ref, part_ref, taps_ref):
    core = core_ref[0]
    put_taps(taps_ref, filters_ref, mixing_ref)
    corr_ref[...] = jnp.zeros_like(corr_ref)
    add_corr(corr_ref, 0, first, fwd, dy_ref, 0)
    add_corr(corr_ref, 1, first, rev, dy_ref, 0)

    def side(b, saved):
        add_corr(corr_ref, b, first, saved, swap_ref, NB)
        for h in range(2):
            cols = columns(h)

            def body(r, carry):
                zero = jnp.zeros((2, STEP // 2, LANES), F32)
                accs = add_filter(taps_ref, ((0, dy_ref, 0), (1, dy_ref, 0), (b, swap_ref, NB)), r, cols, [zero] * NB)
                for n in range(NB):
                    rows = pl.ds(pl.multiple_of(n * BLOCK + r * STEP, STEP), STEP)
                    part_ref[rows, cols] = accs[n].reshape(STEP, LANES)
                return carry

            lax.fori_loop(0, BLOCK // STEP, body, 0)

    @pl.when(core == 0)
    def _():
        side(0, fwd)

    @pl.when(core == 1)
    def _():
        side(1, rev)


def far_kernel(core_ref, right_ref, left_ref, relay_ref, first, fwd, rev, filters_ref, mixing_ref, near_ref, part_ref, sums_ref, grad_ref, corr_ref, taps_ref):
    core = core_ref[0]
    put_taps(taps_ref, filters_ref, mixing_ref)
    corr_ref[...] = near_ref[...]
    add_corr(corr_ref, 0, first, fwd, right_ref, 2 * NB)
    add_corr(corr_ref, 1, first, rev, left_ref, 2 * NB)

    def side(b, saved):
        add_corr(corr_ref, b, first, saved, relay_ref, NB)
        for h in range(2):
            cols = columns(h)

            def body(r, carry):
                def rows(n):
                    return pl.ds(pl.multiple_of(n * BLOCK + r * STEP, STEP), STEP)

                accs = [part_ref[rows(n), cols].reshape(2, STEP // 2, LANES) for n in range(NB)]
                accs = add_filter(taps_ref, ((0, right_ref, 2 * NB), (1, left_ref, 2 * NB), (b, relay_ref, NB)), r, cols, accs)
                for n in range(NB):
                    grad_ref[rows(n), cols] = accs[n].reshape(STEP, LANES).astype(jnp.bfloat16)
                return carry

            lax.fori_loop(0, BLOCK // STEP, body, 0)

    @pl.when(core == 0)
    def _():
        side(1, rev)

    @pl.when(core == 1)
    def _():
        side(0, fwd)

    f, mix, w = weights(filters_ref, mixing_ref)
    filt = [[0.0, 0.0], [0.0, 0.0]]
    mixes = [None] * (LEVELS + 1)
    for level in range(LEVELS):
        d = 2**level
        s = {k: corr_ref[:, ROW[level, k], :] for k in range(0, TAPS, d)}
        for k, wk in w[level].items():
            filt[0][0] = filt[0][0] + wk * s[k + d]
            filt[0][1] = filt[0][1] + wk * s[k]
        filt[1][0] = filt[1][0] + mix[level] * s[d]
        filt[1][1] = filt[1][1] + mix[level] * s[0]
        mixes[level] = f[1][0] * s[d] + f[1][1] * s[0]
        if level == LEVELS - 1:
            mixes[LEVELS] = f[0][0] * s[d] + f[0][1] * s[0]
    sums = [filt[0][0], filt[0][1], filt[1][0], filt[1][1], *mixes]
    for copy in range(sums_ref.shape[0]):
        for b in range(2):
            for j, value in enumerate(sums):
                sums_ref[copy, pl.ds(b * 9 + j, 1), :] = value[b : b + 1]


def specs(n):
    return [pl.BlockSpec(memory_space=pltpu.SMEM)] + [pl.BlockSpec(memory_space=pltpu.VMEM)] * n


def route(value, axes, size, distance):
    pairs = [(i - distance, i) for i in range(size) if 0 <= i - distance < size]
    return lax.ppermute(value, axes, pairs)


def body(level_input, saved_forward, saved_reverse, filters, mixing, cotangent):
    width = level_input.shape[2]
    rows = level_input.shape[1]
    ctx = lax.axis_size(CTX)
    core = lax.axis_index("core")
    dy, first = cotangent[0], level_input[0]
    fwd, rev = saved_forward[:, 0], saved_reverse[:, 0]
    right = route(dy, CTX, ctx, -2)
    left = route(dy, CTX, ctx, 2)
    swap = lax.ppermute(dy, "core", [(0, 1), (1, 0)])
    relay = lax.ppermute(jnp.where(core == 0, right, left), "core", [(0, 1), (1, 0)])
    core_id = core.astype(jnp.int32).reshape(1)
    taps = pltpu.VMEM((2, TAPS, STEP // 2, width), F32)
    params = pltpu.CompilerParams(vmem_limit_bytes=24 * 1024 * 1024)
    near, part = pl.pallas_call(
        near_kernel,
        out_shape=(
            jax.ShapeDtypeStruct((2, ROWS, width), F32),
            jax.ShapeDtypeStruct((rows, width), F32),
        ),
        in_specs=specs(7),
        out_specs=(pl.BlockSpec(memory_space=pltpu.VMEM),) * 2,
        scratch_shapes=[taps],
        compiler_params=params,
        cost_estimate=pl.CostEstimate(flops=30_000_000, bytes_accessed=6_000_000, transcendentals=0),
        name="near",
    )(core_id, dy, swap, first, fwd, rev, filters, mixing)
    sums, grad = pl.pallas_call(
        far_kernel,
        out_shape=(
            jax.ShapeDtypeStruct((8, SUMS, width), F32),
            jax.ShapeDtypeStruct((rows, width), jnp.bfloat16),
        ),
        in_specs=specs(10),
        out_specs=(pl.BlockSpec(memory_space=pltpu.VMEM),) * 2,
        scratch_shapes=[pltpu.VMEM((2, ROWS, width), F32), taps],
        compiler_params=params,
        cost_estimate=pl.CostEstimate(flops=20_000_000, bytes_accessed=6_000_000, transcendentals=0),
        name="far",
    )(core_id, right, left, relay, first, fwd, rev, filters, mixing, near, part)
    groups = (DP, ("y",), ("zh", "core"))
    for i, axes in enumerate(groups):
        got = lax.all_to_all(sums, axes, 0, 0)
        total = jnp.sum(got, axis=0)
        if i + 1 < len(groups):
            sums = jnp.broadcast_to(total[None], sums.shape)
    count = level_input.shape[0] * lax.axis_size(DP) * rows * ctx
    total = (total * (1.0 / math.sqrt(count))).reshape(2, 9, width)
    return grad[None], total[:, :4].reshape(2, 2, 2, width), total[:, 4:]


def solution(mesh):
    fine = Mesh(mesh.devices.reshape(4, 2, 4, 8, 2), DP + CTX)
    return jax.shard_map(
        body,
        mesh=fine,
        in_specs=(
            P(DP, CTX, None),
            P(None, DP, CTX, None),
            P(None, DP, CTX, None),
            P(),
            P(),
            P(DP, CTX, None),
        ),
        out_specs=(P(DP, CTX, None), P(), P()),
        check_vma=False,
    )
```

```python
import math

import jax
import jax.numpy as jnp
from jax import lax
from jax.experimental import pallas as pl
from jax.experimental.pallas import tpu as pltpu
from jax.sharding import Mesh
from jax.sharding import PartitionSpec as P

BLOCK = 128
NB = 8
LEVELS = 4
STEP = 16
LANES = 128
F32 = jnp.float32
DP = ("x", "zl")
CTX = ("zh", "y", "core")
SA, TA, SY, TY = 0, 1, 2, 6
SUMS = 10
ROWS = 16
F00, F01, W0, W8, C0, CD = 0, 1, 2, 3, 4, 7
COEFS = 10


def rows_of(b, n, r):
    block = n if b == 0 else NB - 1 - n
    return pl.ds(pl.multiple_of(block * BLOCK + r * STEP, STEP), STEP)


def wide(value):
    return value.astype(F32).reshape(2, STEP // 2, LANES)


def times(c, v):
    return None if v is None else c * v


def plus(*terms):
    total = None
    for term in terms:
        if term is not None:
            total = term if total is None else total + term
    return total


def share(c, dys, p):
    dy = dys.get
    sums = [None] * SUMS

    def take(row, level, n, value):
        if value is not None:
            sums[row] = plus(sums[row], p(level, n) * value)

    g = {n: plus(times(c[W0], dy(n)), times(c[W8], dy(n + 8))) for n in range(15)}
    for n in range(NB):
        take(SY + 3, 3, n, dy(n + 8))
        take(TY + 3, 3, n, dy(n))
    for level in (2, 1, 0):
        d = 2**level
        for n in range(NB):
            take(SA, level, n, g[n + d])
            take(TA, level, n, g[n])
            take(SY + level, level, n, dy(n + d))
            take(TY + level, level, n, dy(n))
        need = {2: 11, 1: 9, 0: NB}[level]
        g = {
            n: plus(
                times(c[F01], g[n]),
                times(c[F00], g[n + d]),
                times(c[C0 + level], dy(n)),
                times(c[CD + level], dy(n + d)),
            )
            for n in range(need)
        }
    return sums, g


def run(work, first, saved, coef_ref, acc_ref, start, finish):
    for h in range(2):
        cols = pl.ds(h * LANES, LANES)

        def step(r, accs):
            accs = list(accs)
            grads = [start(n, r, cols) for n in range(NB)]
            at = 0
            for b, sources in work:
                c = [coef_ref[b, i, :, cols][None] for i in range(COEFS)]
                dys = {}
                for ref, base in sources:
                    for j in range(NB):
                        if base + j < 23:
                            dys[base + j] = wide(ref[rows_of(b, j, r), cols])

                def p(level, n):
                    rows = rows_of(b, n, r)
                    return wide(first[rows, cols] if level == 0 else saved[b][level - 1, rows, cols])

                sums, g = share(c, dys, p)
                for row in range(SUMS):
                    if sums[row] is not None:
                        accs[at + row] = accs[at + row] + (sums[row][0] + sums[row][1])
                at += SUMS
                for n in range(NB):
                    block = n if b == 0 else NB - 1 - n
                    grads[block] = plus(grads[block], g[n])
            for n in range(NB):
                finish(n, r, cols, grads[n].reshape(STEP, LANES))
            return tuple(accs)

        zero = jnp.zeros((STEP // 2, LANES), F32)
        accs = lax.fori_loop(0, BLOCK // STEP, step, (zero,) * (SUMS * len(work)))
        for i, (b, _) in enumerate(work):
            for row in range(SUMS):
                at = (b, pl.ds(row, 1), cols)
                acc_ref[at] = acc_ref[at] + jnp.sum(accs[i * SUMS + row], axis=0, keepdims=True)


def near_kernel(core_ref, dy_ref, swap_ref, first, fwd, rev, filters_ref, mixing_ref, acc_ref, part_ref, coef_ref):
    core = core_ref[0]
    acc_ref[...] = jnp.zeros_like(acc_ref)
    for b in range(2):
        f = [[filters_ref[b, i, pl.ds(j, 1), :] for j in range(2)] for i in range(2)]
        mix = [mixing_ref[i, pl.ds(b, 1), :] for i in range(LEVELS + 1)]
        c = [None] * COEFS
        c[F00], c[F01] = f[0]
        c[W0] = f[0][1] * mix[4] + f[1][1] * mix[3]
        c[W8] = f[0][0] * mix[4] + f[1][0] * mix[3]
        for level in range(3):
            c[C0 + level] = f[1][1] * mix[level]
            c[CD + level] = f[1][0] * mix[level]
        for i in range(COEFS):
            coef_ref[b, i] = jnp.broadcast_to(c[i], coef_ref.shape[2:])

    def keep(n, r, cols, value):
        part_ref[rows_of(0, n, r), cols] = value

    def side(b):
        own, both = [(dy_ref, 0)], [(dy_ref, 0), (swap_ref, NB)]
        work = [(b, both), (1 - b, own)]
        run(work, first, (fwd, rev), coef_ref, acc_ref, lambda n, r, cols: None, keep)

    for b in range(2):
        pl.when(core == b)(lambda b=b: side(b))


def far_kernel(right_ref, left_ref, first, fwd, rev, coef_ref, near_ref, part_ref, acc_ref, out_ref):
    acc_ref[...] = near_ref[...]

    def start(n, r, cols):
        return part_ref[rows_of(0, n, r), cols].reshape(2, STEP // 2, LANES)

    def keep(n, r, cols, value):
        out_ref[rows_of(0, n, r), cols] = value

    work = [(0, [(right_ref, 2 * NB)]), (1, [(left_ref, 2 * NB)])]
    run(work, first, (fwd, rev), coef_ref, acc_ref, start, keep)


def last_kernel(core_ref, relay_ref, first, fwd, rev, filters_ref, mixing_ref, coef_ref, far_ref, part_ref, sums_ref, grad_ref, acc_ref):
    core = core_ref[0]
    acc_ref[...] = far_ref[...]

    def start(n, r, cols):
        return part_ref[rows_of(0, n, r), cols].reshape(2, STEP // 2, LANES)

    def keep(n, r, cols, value):
        grad_ref[rows_of(0, n, r), cols] = value.astype(grad_ref.dtype)

    for b in range(2):
        work = [(b, [(relay_ref, NB)])]
        pl.when(core == 1 - b)(
            lambda work=work: run(work, first, (fwd, rev), coef_ref, acc_ref, start, keep)
        )
    f = [[filters_ref[:, i, j, :] for j in range(2)] for i in range(2)]
    mix = [mixing_ref[i] for i in range(LEVELS + 1)]
    acc = [acc_ref[:, i, :] for i in range(SUMS)]
    s, t = acc[SY : SY + LEVELS], acc[TY : TY + LEVELS]
    sums = [
        acc[SA] + mix[4] * s[3],
        acc[TA] + mix[4] * t[3],
        sum(mix[i] * s[i] for i in range(LEVELS)),
        sum(mix[i] * t[i] for i in range(LEVELS)),
        *(f[1][0] * s[i] + f[1][1] * t[i] for i in range(LEVELS)),
        f[0][0] * s[3] + f[0][1] * t[3],
    ]
    for copy in range(sums_ref.shape[0]):
        for b in range(2):
            for j, value in enumerate(sums):
                sums_ref[copy, pl.ds(b * 9 + j, 1), :] = value[b : b + 1]


def finish_kernel(factor, got_ref, filters_ref, mixing_ref):
    total = got_ref[0]
    for i in range(1, got_ref.shape[0]):
        total = total + got_ref[i]
    total = total * factor
    for b in range(2):
        for i in range(2):
            for j in range(2):
                at = b * 9 + i * 2 + j
                filters_ref[b, i, pl.ds(j, 1), :] = total[at : at + 1]
        for i in range(LEVELS + 1):
            at = b * 9 + 4 + i
            mixing_ref[i, pl.ds(b, 1), :] = total[at : at + 1]


def call(kernel, name, outs, args, scratch=(), flops=0):
    smem = args[0].dtype == jnp.int32
    vmem = pl.BlockSpec(memory_space=pltpu.VMEM)
    return pl.pallas_call(
        kernel,
        out_shape=outs,
        in_specs=[pl.BlockSpec(memory_space=pltpu.SMEM) if i == 0 and smem else vmem for i in range(len(args))],
        out_specs=(vmem,) * len(outs),
        scratch_shapes=scratch,
        compiler_params=pltpu.CompilerParams(vmem_limit_bytes=24 * 1024 * 1024),
        cost_estimate=pl.CostEstimate(flops=flops, bytes_accessed=6_000_000, transcendentals=0),
        name=name,
    )(*args)


def route(value, axes, size, distance):
    pairs = [(i - distance, i) for i in range(size) if 0 <= i - distance < size]
    return lax.ppermute(value, axes, pairs)


def body(level_input, saved_forward, saved_reverse, filters, mixing, cotangent):
    width = level_input.shape[2]
    rows = level_input.shape[1]
    ctx = lax.axis_size(CTX)
    core = lax.axis_index("core")
    core_id = core.astype(jnp.int32).reshape(1)
    dy = cotangent[0]
    mixing = jnp.swapaxes(mixing, 0, 1)
    inputs = (level_input[0], saved_forward[:, 0], saved_reverse[:, 0])
    acc = jax.ShapeDtypeStruct((2, ROWS, width), F32)
    part = jax.ShapeDtypeStruct((rows, width), F32)
    right = route(dy, CTX, ctx, -2)
    left = route(dy, CTX, ctx, 2)
    swap = lax.ppermute(dy, "core", [(0, 1), (1, 0)])
    acc_near, part_near, coef = call(
        near_kernel,
        "near",
        (acc, part, jax.ShapeDtypeStruct((2, COEFS, STEP // 2, width), F32)),
        (core_id, dy, swap, *inputs, filters, mixing),
        flops=100_000_000,
    )
    right, left, acc_near = lax.optimization_barrier((right, left, acc_near))
    relay = lax.ppermute(jnp.where(core == 0, right, left), "core", [(0, 1), (1, 0)])
    acc_far, part_far = call(
        far_kernel,
        "far",
        (acc, part),
        (right, left, *inputs, coef, acc_near, part_near),
        flops=100_000_000,
    )
    sums, grad = call(
        last_kernel,
        "last",
        (jax.ShapeDtypeStruct((8, 18, width), F32), jax.ShapeDtypeStruct((rows, width), jnp.bfloat16)),
        (core_id, relay, *inputs, filters, mixing, coef, acc_far, part_far),
        scratch=[pltpu.VMEM((2, ROWS, width), F32)],
        flops=100_000_000,
    )
    groups = (("x", "core"), ("y",), ("zl", "zh"))
    for i, axes in enumerate(groups):
        got = lax.all_to_all(sums, axes, 0, 0)
        if i + 1 < len(groups):
            sums = jnp.broadcast_to(jnp.sum(got, axis=0)[None], sums.shape)
    count = level_input.shape[0] * lax.axis_size(DP) * rows * ctx
    grad_filters, grad_mixing = call(
        lambda *refs: finish_kernel(1.0 / math.sqrt(count), *refs),
        "finish",
        (jax.ShapeDtypeStruct(filters.shape, F32), jax.ShapeDtypeStruct(mixing.shape, F32)),
        (got,),
    )
    return grad[None], grad_filters, jnp.swapaxes(grad_mixing, 0, 1)


def solution(mesh):
    fine = Mesh(mesh.devices.reshape(4, 2, 4, 8, 2), DP + CTX)
    return jax.shard_map(
        body,
        mesh=fine,
        in_specs=(
            P(DP, CTX, None),
            P(None, DP, CTX, None),
            P(None, DP, CTX, None),
            P(),
            P(),
            P(DP, CTX, None),
        ),
        out_specs=(P(DP, CTX, None), P(), P()),
        check_vma=False,
    )
```

```python
import math

import jax
import jax.numpy as jnp
from jax import lax
from jax.experimental import pallas as pl
from jax.experimental.pallas import tpu as pltpu
from jax.sharding import Mesh
from jax.sharding import PartitionSpec as P

BLOCK = 128
HEAD = 3 * BLOCK
NB = 8
LEVELS = 4
STEP = 16
LANES = 128
F32 = jnp.float32
DP = ("x", "zl")
CTX = ("zh", "y", "core")
SA, TA, SY, TY = 0, 1, 2, 6
SUMS = 10
ROWS = 16
F00, F01, W0, W8, C0, CD = 0, 1, 2, 3, 4, 7
COEFS = 10


def rows_of(b, n, r):
    block = n if b == 0 else NB - 1 - n
    return pl.ds(pl.multiple_of(block * BLOCK + r * STEP, STEP), STEP)


def wide(value):
    return value.astype(F32).reshape(2, STEP // 2, LANES)


def times(c, v):
    return None if v is None else c * v


def plus(*terms):
    total = None
    for term in terms:
        if term is not None:
            total = term if total is None else total + term
    return total


def share(c, dys, p):
    dy = dys.get
    sums = [None] * SUMS

    def take(row, level, n, value):
        if value is not None:
            sums[row] = plus(sums[row], p(level, n) * value)

    g = {n: plus(times(c[W0], dy(n)), times(c[W8], dy(n + 8))) for n in range(15)}
    for n in range(NB):
        take(SY + 3, 3, n, dy(n + 8))
        take(TY + 3, 3, n, dy(n))
    for level in (2, 1, 0):
        d = 2**level
        for n in range(NB):
            take(SA, level, n, g[n + d])
            take(TA, level, n, g[n])
            take(SY + level, level, n, dy(n + d))
            take(TY + level, level, n, dy(n))
        need = {2: 11, 1: 9, 0: NB}[level]
        g = {
            n: plus(
                times(c[F01], g[n]),
                times(c[F00], g[n + d]),
                times(c[C0 + level], dy(n)),
                times(c[CD + level], dy(n + d)),
            )
            for n in range(need)
        }
    return sums, g


def run(work, saved, coef_ref, acc_ref, start, finish):
    for h in range(2):
        cols = pl.ds(h * LANES, LANES)

        def step(r, accs):
            accs = list(accs)
            grads = [start(n, r, cols) for n in range(NB)]
            at = 0
            for b, sources in work:
                c = [coef_ref[b, i, :, cols][None] for i in range(COEFS)]
                dys = {}
                for ref, base in sources:
                    for j in range(NB):
                        if base + j < 23:
                            dys[base + j] = wide(ref[rows_of(b, j, r), cols])

                def p(level, n):
                    return wide(saved[3 * b + level if level else 0, rows_of(b, n, r), cols])

                sums, g = share(c, dys, p)
                for row in range(SUMS):
                    if sums[row] is not None:
                        accs[at + row] = accs[at + row] + (sums[row][0] + sums[row][1])
                at += SUMS
                for n in range(NB):
                    block = n if b == 0 else NB - 1 - n
                    grads[block] = plus(grads[block], g[n])
            for n in range(NB):
                finish(n, r, cols, grads[n].reshape(STEP, LANES))
            return tuple(accs)

        zero = jnp.zeros((STEP // 2, LANES), F32)
        accs = lax.fori_loop(0, BLOCK // STEP, step, (zero,) * (SUMS * len(work)))
        for i, (b, _) in enumerate(work):
            for row in range(SUMS):
                at = (b, pl.ds(row, 1), cols)
                acc_ref[at] = acc_ref[at] + jnp.sum(accs[i * SUMS + row], axis=0, keepdims=True)


def split_kernel(dy_ref, head_ref, tail_ref, sems):
    head = head_ref.shape[0]
    copies = [
        pltpu.make_async_copy(dy_ref.at[pl.ds(0, head)], head_ref, sems.at[0]),
        pltpu.make_async_copy(dy_ref.at[pl.ds(head, tail_ref.shape[0])], tail_ref, sems.at[1]),
    ]
    for copy in copies:
        copy.start()
    for copy in copies:
        copy.wait()


def near_kernel(core_ref, swap_ref, dy_hbm, first, fwd, rev, filters_hbm, mixing_hbm, acc_ref, part_ref, coef_ref, par_ref, saved, dy_ref, filters_ref, mixing_ref, sems):
    moves = [
        (filters_hbm, filters_ref),
        (mixing_hbm, mixing_ref),
        (dy_hbm, dy_ref),
        (first, saved.at[0]),
        (fwd, saved.at[pl.ds(1, LEVELS - 1)]),
        (rev, saved.at[pl.ds(LEVELS, LEVELS - 1)]),
    ]
    copies = [pltpu.make_async_copy(a, b, sems.at[i]) for i, (a, b) in enumerate(moves)]
    for copy in copies:
        copy.start()
    core = core_ref[0]
    acc_ref[...] = jnp.zeros_like(acc_ref)
    for copy in copies[:2]:
        copy.wait()
    for b in range(2):
        f = [[filters_ref[b, i, pl.ds(j, 1), :] for j in range(2)] for i in range(2)]
        mix = [mixing_ref[i, pl.ds(b, 1), :] for i in range(LEVELS + 1)]
        c = [None] * COEFS
        c[F00], c[F01] = f[0]
        c[W0] = f[0][1] * mix[4] + f[1][1] * mix[3]
        c[W8] = f[0][0] * mix[4] + f[1][0] * mix[3]
        for level in range(3):
            c[C0 + level] = f[1][1] * mix[level]
            c[CD + level] = f[1][0] * mix[level]
        for i in range(COEFS):
            coef_ref[b, i] = jnp.broadcast_to(c[i], coef_ref.shape[2:])
        for i, value in enumerate([*f[0], *f[1], *mix]):
            par_ref[i, pl.ds(b, 1), :] = value
    for copy in copies[2:]:
        copy.wait()

    def keep(n, r, cols, value):
        part_ref[rows_of(0, n, r), cols] = value

    def side(b):
        own, both = [(dy_ref, 0)], [(dy_ref, 0), (swap_ref, NB)]
        work = [(b, both), (1 - b, own)]
        run(work, saved, coef_ref, acc_ref, lambda n, r, cols: None, keep)

    for b in range(2):
        pl.when(core == b)(lambda b=b: side(b))


def far_kernel(right_ref, left_ref, saved, coef_ref, near_ref, part_ref, acc_ref, out_ref):
    acc_ref[...] = near_ref[...]

    def start(n, r, cols):
        return part_ref[rows_of(0, n, r), cols].reshape(2, STEP // 2, LANES)

    def keep(n, r, cols, value):
        out_ref[rows_of(0, n, r), cols] = value

    work = [(0, [(right_ref, 2 * NB)]), (1, [(left_ref, 2 * NB)])]
    run(work, saved, coef_ref, acc_ref, start, keep)


def last_kernel(core_ref, relay_ref, saved, par_ref, coef_ref, far_ref, part_ref, sums_ref, grad_ref, acc_ref):
    core = core_ref[0]
    acc_ref[...] = far_ref[...]

    def start(n, r, cols):
        return part_ref[rows_of(0, n, r), cols].reshape(2, STEP // 2, LANES)

    def keep(n, r, cols, value):
        grad_ref[rows_of(0, n, r), cols] = value.astype(grad_ref.dtype)

    for b in range(2):
        work = [(b, [(relay_ref, NB)])]
        pl.when(core == 1 - b)(
            lambda work=work: run(work, saved, coef_ref, acc_ref, start, keep)
        )
    f = [[par_ref[2 * i + j] for j in range(2)] for i in range(2)]
    mix = [par_ref[4 + i] for i in range(LEVELS + 1)]
    acc = [acc_ref[:, i, :] for i in range(SUMS)]
    s, t = acc[SY : SY + LEVELS], acc[TY : TY + LEVELS]
    sums = [
        acc[SA] + mix[4] * s[3],
        acc[TA] + mix[4] * t[3],
        sum(mix[i] * s[i] for i in range(LEVELS)),
        sum(mix[i] * t[i] for i in range(LEVELS)),
        *(f[1][0] * s[i] + f[1][1] * t[i] for i in range(LEVELS)),
        f[0][0] * s[3] + f[0][1] * t[3],
    ]
    for copy in range(sums_ref.shape[0]):
        for b in range(2):
            for j, value in enumerate(sums):
                for h in range(2):
                    at = 2 * (b * 9 + j) + h
                    sums_ref[copy, pl.ds(at, 1), :] = value[b : b + 1, h * LANES : (h + 1) * LANES]


def finish_kernel(factor, got_ref, filters_ref, mixing_ref):
    total = got_ref[0]
    for i in range(1, got_ref.shape[0]):
        total = total + got_ref[i]
    total = total * factor
    for b in range(2):
        for j in range(9):
            for h in range(2):
                row = total[2 * (b * 9 + j) + h : 2 * (b * 9 + j) + h + 1]
                cols = pl.ds(h * LANES, LANES)
                if j < 4:
                    filters_ref[b, j // 2, pl.ds(j % 2, 1), cols] = row
                else:
                    mixing_ref[j - 4, pl.ds(b, 1), cols] = row


def call(kernel, name, outs, args, spaces, scratch=(), flops=0):
    space = {"s": pltpu.SMEM, "v": pltpu.VMEM, "h": pltpu.HBM}
    args = [pltpu.with_memory_space_constraint(a, pltpu.HBM) if k == "h" else a for a, k in zip(args, spaces)]
    return pl.pallas_call(
        kernel,
        out_shape=outs,
        in_specs=[pl.BlockSpec(memory_space=space[k]) for k in spaces],
        out_specs=(pl.BlockSpec(memory_space=pltpu.VMEM),) * len(outs),
        scratch_shapes=scratch,
        compiler_params=pltpu.CompilerParams(vmem_limit_bytes=24 * 1024 * 1024),
        cost_estimate=pl.CostEstimate(flops=flops, bytes_accessed=6_000_000, transcendentals=0),
        name=name,
    )(*args)


def routes():
    zs, ys, cores = (lax.axis_size(axis) for axis in CTX)

    def at(z, y, c):
        return (z * ys + y) * cores + c

    spots = [(z, c) for z in range(zs) for c in range(cores)]
    inner = [(at(z, y, c), at(z, y + 1, c)) for z, c in spots for y in range(ys - 1)]
    cross = [(at(z, ys - 1, c), at(z + 1, 0, c)) for z, c in spots if z + 1 < zs]
    hop = [(at(z, ys - 1, c), at(z + 1, ys - 1, c)) for z, c in spots if z + 1 < zs]
    hop += [(at(z + 1, 0, c), at(z, 0, c)) for z, c in spots if z + 1 < zs]
    turn_left = [(at(z + 1, ys - 1, c), at(z + 1, 0, c)) for z, c in spots if z + 1 < zs]
    turn_right = [(at(z, 0, c), at(z, ys - 1, c)) for z, c in spots if z + 1 < zs]
    back = [(b, a) for a, b in inner]
    return hop, inner + cross, back + [(b, a) for a, b in cross], inner + turn_left, back + turn_right


def body(level_input, saved_forward, saved_reverse, filters, mixing, cotangent):
    width = level_input.shape[2]
    rows = level_input.shape[1]
    ctx = lax.axis_size(CTX)
    core = lax.axis_index("core")
    core_id = core.astype(jnp.int32).reshape(1)
    dy = cotangent[0]
    mixing = jnp.swapaxes(mixing, 0, 1)
    acc = jax.ShapeDtypeStruct((2, ROWS, width), F32)
    part = jax.ShapeDtypeStruct((rows, width), F32)
    pair = [(0, 1), (1, 0)]
    hop, left_tail, right_tail, left_head, right_head = routes()
    head, tail = call(
        split_kernel,
        "split",
        tuple(jax.ShapeDtypeStruct((n, width), dy.dtype) for n in (HEAD, rows - HEAD)),
        (dy,),
        "h",
        scratch=[pltpu.SemaphoreType.DMA((2,))],
    )
    dy, head, tail = lax.optimization_barrier((dy, head, tail))
    hopped = lax.ppermute(head, CTX, hop)
    left5 = lax.ppermute(tail, CTX, left_tail)
    right5 = lax.ppermute(tail, CTX, right_tail)
    swap = lax.ppermute(dy, "core", pair)
    row = lax.axis_index("y")
    left3 = lax.ppermute(jnp.where(row == lax.axis_size("y") - 1, hopped, head), CTX, left_head)
    right3 = lax.ppermute(jnp.where(row == 0, hopped, head), CTX, right_head)
    acc_near, part_near, coef, par, saved = call(
        near_kernel,
        "near",
        (
            acc,
            part,
            jax.ShapeDtypeStruct((2, COEFS, STEP // 2, width), F32),
            jax.ShapeDtypeStruct((LEVELS + 5, 2, width), F32),
            jax.ShapeDtypeStruct((2 * LEVELS - 1, rows, width), dy.dtype),
        ),
        (core_id, swap, dy, level_input[0], saved_forward[:, 0], saved_reverse[:, 0], filters, mixing),
        "svhhhhhh",
        scratch=[
            pltpu.VMEM((rows, width), dy.dtype),
            pltpu.VMEM(filters.shape, F32),
            pltpu.VMEM(mixing.shape, F32),
            pltpu.SemaphoreType.DMA((6,)),
        ],
        flops=20_000_000,
    )
    left3, left5, right3, right5, acc_near = lax.optimization_barrier((left3, left5, right3, right5, acc_near))
    left = jnp.concatenate([left3, left5])
    right = jnp.concatenate([right3, right5])
    relay = lax.ppermute(jnp.where(core == 0, right, left), "core", pair)
    acc_far, part_far = call(
        far_kernel,
        "far",
        (acc, part),
        (right, left, saved, coef, acc_near, part_near),
        "vvvvvv",
        flops=20_000_000,
    )
    sums, grad = call(
        last_kernel,
        "last",
        (jax.ShapeDtypeStruct((8, 18 * width // LANES, LANES), F32), jax.ShapeDtypeStruct((rows, width), jnp.bfloat16)),
        (core_id, relay, saved, par, coef, acc_far, part_far),
        "svvvvvv",
        scratch=[pltpu.VMEM((2, ROWS, width), F32)],
        flops=20_000_000,
    )
    groups = (("x", "core"), ("y",), ("zl", "zh"))
    for i, axes in enumerate(groups):
        got = lax.all_to_all(sums, axes, 0, 0)
        if i + 1 < len(groups):
            sums = jnp.broadcast_to(jnp.sum(got, axis=0)[None], sums.shape)
    count = level_input.shape[0] * lax.axis_size(DP) * rows * ctx
    grad_filters, grad_mixing = call(
        lambda *refs: finish_kernel(1.0 / math.sqrt(count), *refs),
        "finish",
        (jax.ShapeDtypeStruct(filters.shape, F32), jax.ShapeDtypeStruct(mixing.shape, F32)),
        (got,),
        "v",
    )
    return grad[None], grad_filters, jnp.swapaxes(grad_mixing, 0, 1)


def solution(mesh):
    fine = Mesh(mesh.devices.reshape(4, 2, 4, 8, 2), DP + CTX)
    return jax.shard_map(
        body,
        mesh=fine,
        in_specs=(
            P(DP, CTX, None),
            P(None, DP, CTX, None),
            P(None, DP, CTX, None),
            P(),
            P(),
            P(DP, CTX, None),
        ),
        out_specs=(P(DP, CTX, None), P(), P()),
        check_vma=False,
    )
```

```python
import math

import jax
import jax.numpy as jnp
from jax import lax
from jax.experimental import pallas as pl
from jax.experimental.pallas import tpu as pltpu
from jax.sharding import Mesh
from jax.sharding import PartitionSpec as P

BLOCK = 128
HEAD = 3 * BLOCK
NB = 8
LEVELS = 4
STEP = 16
LANES = 128
F32 = jnp.float32
DP = ("x", "zl")
CTX = ("zh", "y", "core")
SA, TA, SY, TY = 0, 1, 2, 6
SUMS = 10
ROWS = 16
F00, F01, W0, W8, C0, CD = 0, 1, 2, 3, 4, 7
COEFS = 10


def rows_of(b, n, r):
    block = n if b == 0 else NB - 1 - n
    return pl.ds(pl.multiple_of(block * BLOCK + r * STEP, STEP), STEP)


def wide(value):
    return value.astype(F32).reshape(2, STEP // 2, LANES)


def times(c, v):
    return None if v is None else c * v


def plus(*terms):
    total = None
    for term in terms:
        if term is not None:
            total = term if total is None else total + term
    return total


def share(c, dys, p):
    dy = dys.get
    sums = [None] * SUMS

    def take(row, level, n, value):
        if value is not None:
            sums[row] = plus(sums[row], p(level, n) * value)

    g = {n: plus(times(c[W0], dy(n)), times(c[W8], dy(n + 8))) for n in range(15)}
    for n in range(NB):
        take(SY + 3, 3, n, dy(n + 8))
        take(TY + 3, 3, n, dy(n))
    for level in (2, 1, 0):
        d = 2**level
        for n in range(NB):
            take(SA, level, n, g[n + d])
            take(TA, level, n, g[n])
            take(SY + level, level, n, dy(n + d))
            take(TY + level, level, n, dy(n))
        need = {2: 11, 1: 9, 0: NB}[level]
        g = {
            n: plus(
                times(c[F01], g[n]),
                times(c[F00], g[n + d]),
                times(c[C0 + level], dy(n)),
                times(c[CD + level], dy(n + d)),
            )
            for n in range(need)
        }
    return sums, g


def run(work, saved, coef_ref, acc_ref, start, finish):
    for h in range(2):
        cols = pl.ds(h * LANES, LANES)

        def step(r, accs):
            accs = list(accs)
            grads = [start(n, r, cols) for n in range(NB)]
            at = 0
            for b, sources in work:
                c = [coef_ref[b, i, :, cols][None] for i in range(COEFS)]
                dys = {}
                for ref, base in sources:
                    for j in range(NB):
                        if base + j < 23:
                            dys[base + j] = wide(ref[rows_of(b, j, r), cols])

                def p(level, n):
                    return wide(saved[3 * b + level if level else 0, rows_of(b, n, r), cols])

                sums, g = share(c, dys, p)
                for row in range(SUMS):
                    if sums[row] is not None:
                        accs[at + row] = accs[at + row] + (sums[row][0] + sums[row][1])
                at += SUMS
                for n in range(NB):
                    block = n if b == 0 else NB - 1 - n
                    grads[block] = plus(grads[block], g[n])
            for n in range(NB):
                finish(n, r, cols, grads[n].reshape(STEP, LANES))
            return tuple(accs)

        zero = jnp.zeros((STEP // 2, LANES), F32)
        accs = lax.fori_loop(0, BLOCK // STEP, step, (zero,) * (SUMS * len(work)))
        for i, (b, _) in enumerate(work):
            for row in range(SUMS):
                at = (b, pl.ds(row, 1), cols)
                acc_ref[at] = acc_ref[at] + jnp.sum(accs[i * SUMS + row], axis=0, keepdims=True)


def split_kernel(dy_ref, head_ref, tail_ref, sems):
    head = head_ref.shape[0]
    copies = [
        pltpu.make_async_copy(dy_ref.at[pl.ds(0, head)], head_ref, sems.at[0]),
        pltpu.make_async_copy(dy_ref.at[pl.ds(head, tail_ref.shape[0])], tail_ref, sems.at[1]),
    ]
    for copy in copies:
        copy.start()
    for copy in copies:
        copy.wait()


def near_kernel(dy_hbm, first, fwd, rev, filters_hbm, mixing_hbm, acc_ref, part_ref, coef_ref, par_ref, saved, dy_ref, filters_ref, mixing_ref, sems):
    moves = [
        (filters_hbm, filters_ref),
        (mixing_hbm, mixing_ref),
        (dy_hbm, dy_ref),
        (first, saved.at[0]),
        (fwd, saved.at[pl.ds(1, LEVELS - 1)]),
        (rev, saved.at[pl.ds(LEVELS, LEVELS - 1)]),
    ]
    copies = [pltpu.make_async_copy(a, b, sems.at[i]) for i, (a, b) in enumerate(moves)]
    for copy in copies:
        copy.start()
    acc_ref[...] = jnp.zeros_like(acc_ref)
    for copy in copies[:2]:
        copy.wait()
    for b in range(2):
        f = [[filters_ref[b, i, pl.ds(j, 1), :] for j in range(2)] for i in range(2)]
        mix = [mixing_ref[i, pl.ds(b, 1), :] for i in range(LEVELS + 1)]
        c = [None] * COEFS
        c[F00], c[F01] = f[0]
        c[W0] = f[0][1] * mix[4] + f[1][1] * mix[3]
        c[W8] = f[0][0] * mix[4] + f[1][0] * mix[3]
        for level in range(3):
            c[C0 + level] = f[1][1] * mix[level]
            c[CD + level] = f[1][0] * mix[level]
        for i in range(COEFS):
            coef_ref[b, i] = jnp.broadcast_to(c[i], coef_ref.shape[2:])
        for i, value in enumerate([*f[0], *f[1], *mix]):
            par_ref[i, pl.ds(b, 1), :] = value
    for copy in copies[2:]:
        copy.wait()

    def keep(n, r, cols, value):
        part_ref[rows_of(0, n, r), cols] = value

    work = [(0, [(dy_ref, 0)]), (1, [(dy_ref, 0)])]
    run(work, saved, coef_ref, acc_ref, lambda n, r, cols: None, keep)


def far_kernel(core_ref, swap_ref, right_ref, left_ref, saved, coef_ref, near_ref, part_ref, acc_ref, out_ref):
    core = core_ref[0]
    acc_ref[...] = near_ref[...]

    def start(n, r, cols):
        return part_ref[rows_of(0, n, r), cols].reshape(2, STEP // 2, LANES)

    def keep(n, r, cols, value):
        out_ref[rows_of(0, n, r), cols] = value

    for b in range(2):
        far = [[(right_ref, 2 * NB)], [(left_ref, 2 * NB)]]
        far[b] = [(swap_ref, NB)] + far[b]
        work = list(enumerate(far))
        pl.when(core == b)(lambda work=work: run(work, saved, coef_ref, acc_ref, start, keep))


def last_kernel(core_ref, relay_ref, saved, par_ref, coef_ref, far_ref, part_ref, sums_ref, grad_ref, acc_ref):
    core = core_ref[0]
    acc_ref[...] = far_ref[...]

    def start(n, r, cols):
        return part_ref[rows_of(0, n, r), cols].reshape(2, STEP // 2, LANES)

    def keep(n, r, cols, value):
        grad_ref[rows_of(0, n, r), cols] = value.astype(grad_ref.dtype)

    for b in range(2):
        work = [(b, [(relay_ref, NB)])]
        pl.when(core == 1 - b)(
            lambda work=work: run(work, saved, coef_ref, acc_ref, start, keep)
        )
    f = [[par_ref[2 * i + j] for j in range(2)] for i in range(2)]
    mix = [par_ref[4 + i] for i in range(LEVELS + 1)]
    acc = [acc_ref[:, i, :] for i in range(SUMS)]
    s, t = acc[SY : SY + LEVELS], acc[TY : TY + LEVELS]
    sums = [
        acc[SA] + mix[4] * s[3],
        acc[TA] + mix[4] * t[3],
        sum(mix[i] * s[i] for i in range(LEVELS)),
        sum(mix[i] * t[i] for i in range(LEVELS)),
        *(f[1][0] * s[i] + f[1][1] * t[i] for i in range(LEVELS)),
        f[0][0] * s[3] + f[0][1] * t[3],
    ]
    for b in range(2):
        for j, value in enumerate(sums):
            for h in range(2):
                at = 2 * (b * 9 + j) + h
                sums_ref[0, pl.ds(at, 1), :] = value[b : b + 1, h * LANES : (h + 1) * LANES]
    for copy in range(1, sums_ref.shape[0]):
        sums_ref[copy] = sums_ref[0]


def finish_kernel(factor, got_ref, filters_ref, mixing_ref):
    total = got_ref[0]
    for i in range(1, got_ref.shape[0]):
        total = total + got_ref[i]
    total = total * factor
    for b in range(2):
        for j in range(9):
            for h in range(2):
                row = total[2 * (b * 9 + j) + h : 2 * (b * 9 + j) + h + 1]
                cols = pl.ds(h * LANES, LANES)
                if j < 4:
                    filters_ref[b, j // 2, pl.ds(j % 2, 1), cols] = row
                else:
                    mixing_ref[j - 4, pl.ds(b, 1), cols] = row


def call(kernel, name, outs, args, spaces, scratch=(), flops=0):
    space = {"s": pltpu.SMEM, "v": pltpu.VMEM, "h": pltpu.HBM}
    args = [pltpu.with_memory_space_constraint(a, pltpu.HBM) if k == "h" else a for a, k in zip(args, spaces)]
    return pl.pallas_call(
        kernel,
        out_shape=outs,
        in_specs=[pl.BlockSpec(memory_space=space[k]) for k in spaces],
        out_specs=(pl.BlockSpec(memory_space=pltpu.VMEM),) * len(outs),
        scratch_shapes=scratch,
        compiler_params=pltpu.CompilerParams(vmem_limit_bytes=24 * 1024 * 1024),
        cost_estimate=pl.CostEstimate(flops=flops, bytes_accessed=6_000_000, transcendentals=0),
        name=name,
    )(*args)


def routes():
    zs, ys, cores = (lax.axis_size(axis) for axis in CTX)

    def at(z, y, c):
        return (z * ys + y) * cores + c

    spots = [(z, c) for z in range(zs) for c in range(cores)]
    seams = [(z, c) for z, c in spots if z + 1 < zs]
    end = ys - 1
    inner = [(at(z, y, c), at(z, y + 1, c)) for z, c in spots for y in range(end)]
    cross = [(at(z, end, c), at(z + 1, 0, c)) for z, c in seams]
    cross += [(at(z + 1, 0, c), at(z, end, c)) for z, c in seams]
    hop = [(at(z, end, c), at(z + 1, end, c)) for z, c in seams]
    hop += [(at(z + 1, 0, c), at(z, 0, c)) for z, c in seams]
    turn = [(at(z + 1, end, c), at(z + 1, 0, c)) for z, c in seams]
    turn += [(at(z, 0, c), at(z, end, c)) for z, c in seams]
    return inner, cross, hop, turn


def body(level_input, saved_forward, saved_reverse, filters, mixing, cotangent):
    width = level_input.shape[2]
    rows = level_input.shape[1]
    ctx = lax.axis_size(CTX)
    core = lax.axis_index("core")
    core_id = core.astype(jnp.int32).reshape(1)
    dy = cotangent[0]
    mixing = jnp.swapaxes(mixing, 0, 1)
    acc = jax.ShapeDtypeStruct((2, ROWS, width), F32)
    part = jax.ShapeDtypeStruct((rows, width), F32)
    pair = [(0, 1), (1, 0)]
    inner, cross, hop, turn = routes()
    head, tail = call(
        split_kernel,
        "split",
        tuple(jax.ShapeDtypeStruct((n, width), dy.dtype) for n in (HEAD, rows - HEAD)),
        (dy,),
        "h",
        scratch=[pltpu.SemaphoreType.DMA((2,))],
    )
    hopped = lax.ppermute(head, CTX, hop)
    crossed = lax.ppermute(tail, CTX, cross)
    left = lax.ppermute(dy, CTX, inner)
    right = lax.ppermute(dy, CTX, [(b, a) for a, b in inner])
    swap = lax.ppermute(dy, "core", pair)
    own, hopped = lax.optimization_barrier((dy, hopped))
    turned = lax.ppermute(hopped, CTX, turn)
    acc_near, part_near, coef, par, saved = call(
        near_kernel,
        "near",
        (
            acc,
            part,
            jax.ShapeDtypeStruct((2, COEFS, STEP // 2, width), F32),
            jax.ShapeDtypeStruct((LEVELS + 5, 2, width), F32),
            jax.ShapeDtypeStruct((2 * LEVELS - 1, rows, width), dy.dtype),
        ),
        (own, level_input[0], saved_forward[:, 0], saved_reverse[:, 0], filters, mixing),
        "hhhhhh",
        scratch=[
            pltpu.VMEM((rows, width), dy.dtype),
            pltpu.VMEM(filters.shape, F32),
            pltpu.VMEM(mixing.shape, F32),
            pltpu.SemaphoreType.DMA((6,)),
        ],
        flops=20_000_000,
    )
    left, right, turned, crossed, acc_near = lax.optimization_barrier((left, right, turned, crossed, acc_near))
    row = lax.axis_index("y")
    detour = jnp.concatenate([turned, crossed])
    left = jnp.where(row == 0, detour, left)
    right = jnp.where(row == lax.axis_size("y") - 1, detour, right)
    relay = lax.ppermute(jnp.where(core == 0, right, left), "core", pair)
    acc_far, part_far = call(
        far_kernel,
        "far",
        (acc, part),
        (core_id, swap, right, left, saved, coef, acc_near, part_near),
        "svvvvvvv",
        flops=20_000_000,
    )
    sums, grad = call(
        last_kernel,
        "last",
        (jax.ShapeDtypeStruct((8, 18 * width // LANES, LANES), F32), jax.ShapeDtypeStruct((rows, width), jnp.bfloat16)),
        (core_id, relay, saved, par, coef, acc_far, part_far),
        "svvvvvv",
        scratch=[pltpu.VMEM((2, ROWS, width), F32)],
        flops=20_000_000,
    )
    groups = (("x", "core"), ("y",), ("zl", "zh"))
    for i, axes in enumerate(groups):
        got = lax.all_to_all(sums, axes, 0, 0)
        if i + 1 < len(groups):
            sums = jnp.broadcast_to(jnp.sum(got, axis=0)[None], sums.shape)
    count = level_input.shape[0] * lax.axis_size(DP) * rows * ctx
    grad_filters, grad_mixing = call(
        lambda *refs: finish_kernel(1.0 / math.sqrt(count), *refs),
        "finish",
        (jax.ShapeDtypeStruct(filters.shape, F32), jax.ShapeDtypeStruct(mixing.shape, F32)),
        (got,),
        "v",
    )
    return grad[None], grad_filters, jnp.swapaxes(grad_mixing, 0, 1)


def solution(mesh):
    fine = Mesh(mesh.devices.reshape(4, 2, 4, 8, 2), DP + CTX)
    return jax.shard_map(
        body,
        mesh=fine,
        in_specs=(
            P(DP, CTX, None),
            P(None, DP, CTX, None),
            P(None, DP, CTX, None),
            P(),
            P(),
            P(DP, CTX, None),
        ),
        out_specs=(P(DP, CTX, None), P(), P()),
        check_vma=False,
    )
```

```python
import math

import jax
import jax.numpy as jnp
from jax import lax
from jax.experimental import pallas as pl
from jax.experimental.pallas import tpu as pltpu
from jax.sharding import Mesh
from jax.sharding import PartitionSpec as P

BLOCK = 128
HEAD = 2 * BLOCK
NB = 8
LEVELS = 4
STEP = 16
LANES = 128
F32 = jnp.float32
DP = ("x", "zl")
CTX = ("zh", "y", "core")
SA, TA, SY, TY = 0, 1, 2, 6
SUMS = 10
ROWS = 16
F00, F01, W0, W8, C0, CD = 0, 1, 2, 3, 4, 7
COEFS = 10


def rows_of(b, n, r):
    block = n if b == 0 else NB - 1 - n
    return pl.ds(pl.multiple_of(block * BLOCK + r * STEP, STEP), STEP)


def wide(value):
    return value.astype(F32).reshape(2, STEP // 2, LANES)


def times(c, v):
    return None if v is None else c * v


def plus(*terms):
    total = None
    for term in terms:
        if term is not None:
            total = term if total is None else total + term
    return total


def share(c, dys, p):
    dy = dys.get
    sums = [None] * SUMS

    def take(row, level, n, value):
        if value is not None:
            sums[row] = plus(sums[row], p(level, n) * value)

    g = {n: plus(times(c[W0], dy(n)), times(c[W8], dy(n + 8))) for n in range(15)}
    for n in range(NB):
        take(SY + 3, 3, n, dy(n + 8))
        take(TY + 3, 3, n, dy(n))
    for level in (2, 1, 0):
        d = 2**level
        for n in range(NB):
            take(SA, level, n, g[n + d])
            take(TA, level, n, g[n])
            take(SY + level, level, n, dy(n + d))
            take(TY + level, level, n, dy(n))
        need = {2: 11, 1: 9, 0: NB}[level]
        g = {
            n: plus(
                times(c[F01], g[n]),
                times(c[F00], g[n + d]),
                times(c[C0 + level], dy(n)),
                times(c[CD + level], dy(n + d)),
            )
            for n in range(need)
        }
    return sums, g


def run(work, saved, coef_ref, acc_ref, start, finish):
    for h in range(2):
        cols = pl.ds(h * LANES, LANES)

        def step(r, accs):
            accs = list(accs)
            grads = [start(n, r, cols) for n in range(NB)]
            at = 0
            for b, sources in work:
                c = [coef_ref[b, i, :, cols][None] for i in range(COEFS)]
                dys = {}
                for ref, base in sources:
                    for j in range(NB):
                        if base + j < 23:
                            dys[base + j] = wide(ref[rows_of(b, j, r), cols])

                def p(level, n):
                    return wide(saved[3 * b + level if level else 0, rows_of(b, n, r), cols])

                sums, g = share(c, dys, p)
                for row in range(SUMS):
                    if sums[row] is not None:
                        accs[at + row] = accs[at + row] + (sums[row][0] + sums[row][1])
                at += SUMS
                for n in range(NB):
                    block = n if b == 0 else NB - 1 - n
                    grads[block] = plus(grads[block], g[n])
            for n in range(NB):
                finish(n, r, cols, grads[n].reshape(STEP, LANES))
            return tuple(accs)

        zero = jnp.zeros((STEP // 2, LANES), F32)
        accs = lax.fori_loop(0, BLOCK // STEP, step, (zero,) * (SUMS * len(work)))
        for i, (b, _) in enumerate(work):
            for row in range(SUMS):
                at = (b, pl.ds(row, 1), cols)
                acc_ref[at] = acc_ref[at] + jnp.sum(accs[i * SUMS + row], axis=0, keepdims=True)


def split_kernel(dy_ref, head_ref, tail_ref, sems):
    head = head_ref.shape[0]
    copies = [
        pltpu.make_async_copy(dy_ref.at[pl.ds(0, head)], head_ref, sems.at[0]),
        pltpu.make_async_copy(dy_ref.at[pl.ds(head, tail_ref.shape[0])], tail_ref, sems.at[1]),
    ]
    for copy in copies:
        copy.start()
    for copy in copies:
        copy.wait()


def near_kernel(dy_hbm, first, fwd, rev, filters_hbm, mixing_hbm, acc_ref, part_ref, coef_ref, par_ref, saved, dy_ref, filters_ref, mixing_ref, sems):
    moves = [
        (filters_hbm, filters_ref),
        (mixing_hbm, mixing_ref),
        (dy_hbm, dy_ref),
        (first, saved.at[0]),
        (fwd, saved.at[pl.ds(1, LEVELS - 1)]),
        (rev, saved.at[pl.ds(LEVELS, LEVELS - 1)]),
    ]
    copies = [pltpu.make_async_copy(a, b, sems.at[i]) for i, (a, b) in enumerate(moves)]
    for copy in copies:
        copy.start()
    acc_ref[...] = jnp.zeros_like(acc_ref)
    for copy in copies[:2]:
        copy.wait()
    for b in range(2):
        f = [[filters_ref[b, i, pl.ds(j, 1), :] for j in range(2)] for i in range(2)]
        mix = [mixing_ref[i, pl.ds(b, 1), :] for i in range(LEVELS + 1)]
        c = [None] * COEFS
        c[F00], c[F01] = f[0]
        c[W0] = f[0][1] * mix[4] + f[1][1] * mix[3]
        c[W8] = f[0][0] * mix[4] + f[1][0] * mix[3]
        for level in range(3):
            c[C0 + level] = f[1][1] * mix[level]
            c[CD + level] = f[1][0] * mix[level]
        for i in range(COEFS):
            coef_ref[b, i] = jnp.broadcast_to(c[i], coef_ref.shape[2:])
        for i, value in enumerate([*f[0], *f[1], *mix]):
            par_ref[i, pl.ds(b, 1), :] = value
    for copy in copies[2:]:
        copy.wait()

    def keep(n, r, cols, value):
        part_ref[rows_of(0, n, r), cols] = value

    work = [(0, [(dy_ref, 0)]), (1, [(dy_ref, 0)])]
    run(work, saved, coef_ref, acc_ref, lambda n, r, cols: None, keep)


def far_kernel(core_ref, swap_ref, right_ref, left_ref, saved, coef_ref, near_ref, part_ref, acc_ref, out_ref):
    core = core_ref[0]
    acc_ref[...] = near_ref[...]

    def start(n, r, cols):
        return part_ref[rows_of(0, n, r), cols].reshape(2, STEP // 2, LANES)

    def keep(n, r, cols, value):
        out_ref[rows_of(0, n, r), cols] = value

    for b in range(2):
        far = [[(right_ref, 2 * NB)], [(left_ref, 2 * NB)]]
        far[b] = [(swap_ref, NB)] + far[b]
        work = list(enumerate(far))
        pl.when(core == b)(lambda work=work: run(work, saved, coef_ref, acc_ref, start, keep))


def last_kernel(core_ref, relay_ref, saved, par_ref, coef_ref, far_ref, part_ref, sums_ref, grad_ref, acc_ref):
    core = core_ref[0]
    acc_ref[...] = far_ref[...]

    def start(n, r, cols):
        return part_ref[rows_of(0, n, r), cols].reshape(2, STEP // 2, LANES)

    def keep(n, r, cols, value):
        grad_ref[rows_of(0, n, r), cols] = value.astype(grad_ref.dtype)

    for b in range(2):
        work = [(b, [(relay_ref, NB)])]
        pl.when(core == 1 - b)(
            lambda work=work: run(work, saved, coef_ref, acc_ref, start, keep)
        )
    f = [[par_ref[2 * i + j] for j in range(2)] for i in range(2)]
    mix = [par_ref[4 + i] for i in range(LEVELS + 1)]
    acc = [acc_ref[:, i, :] for i in range(SUMS)]
    s, t = acc[SY : SY + LEVELS], acc[TY : TY + LEVELS]
    sums = [
        acc[SA] + mix[4] * s[3],
        acc[TA] + mix[4] * t[3],
        sum(mix[i] * s[i] for i in range(LEVELS)),
        sum(mix[i] * t[i] for i in range(LEVELS)),
        *(f[1][0] * s[i] + f[1][1] * t[i] for i in range(LEVELS)),
        f[0][0] * s[3] + f[0][1] * t[3],
    ]
    for b in range(2):
        for j, value in enumerate(sums):
            for h in range(2):
                at = 2 * (b * 9 + j) + h
                sums_ref[0, pl.ds(at, 1), :] = value[b : b + 1, h * LANES : (h + 1) * LANES]
    for copy in range(1, sums_ref.shape[0]):
        sums_ref[copy] = sums_ref[0]


def finish_kernel(factor, got_ref, filters_ref, mixing_ref):
    total = got_ref[0]
    for i in range(1, got_ref.shape[0]):
        total = total + got_ref[i]
    total = total * factor
    for b in range(2):
        for j in range(9):
            for h in range(2):
                row = total[2 * (b * 9 + j) + h : 2 * (b * 9 + j) + h + 1]
                cols = pl.ds(h * LANES, LANES)
                if j < 4:
                    filters_ref[b, j // 2, pl.ds(j % 2, 1), cols] = row
                else:
                    mixing_ref[j - 4, pl.ds(b, 1), cols] = row


def call(kernel, name, outs, args, spaces, scratch=(), flops=0):
    space = {"s": pltpu.SMEM, "v": pltpu.VMEM, "h": pltpu.HBM}
    args = [pltpu.with_memory_space_constraint(a, pltpu.HBM) if k == "h" else a for a, k in zip(args, spaces)]
    return pl.pallas_call(
        kernel,
        out_shape=outs,
        in_specs=[pl.BlockSpec(memory_space=space[k]) for k in spaces],
        out_specs=(pl.BlockSpec(memory_space=pltpu.VMEM),) * len(outs),
        scratch_shapes=scratch,
        compiler_params=pltpu.CompilerParams(vmem_limit_bytes=24 * 1024 * 1024),
        cost_estimate=pl.CostEstimate(flops=flops, bytes_accessed=6_000_000, transcendentals=0),
        name=name,
    )(*args)


def routes():
    zs, ys, cores = (lax.axis_size(axis) for axis in CTX)

    def at(z, y, c):
        return (z * ys + y) * cores + c

    spots = [(z, c) for z in range(zs) for c in range(cores)]
    seams = [(z, c) for z, c in spots if z + 1 < zs]
    end = ys - 1
    inner = [(at(z, y, c), at(z, y + 1, c)) for z, c in spots for y in range(end)]
    cross = [(at(z, end, c), at(z + 1, 0, c)) for z, c in seams]
    cross += [(at(z + 1, 0, c), at(z, end, c)) for z, c in seams]
    hop = [(at(z, end, c), at(z + 1, end, c)) for z, c in seams]
    hop += [(at(z + 1, 0, c), at(z, 0, c)) for z, c in seams]
    turn = [(at(z + 1, end, c), at(z + 1, 0, c)) for z, c in seams]
    turn += [(at(z, 0, c), at(z, end, c)) for z, c in seams]
    return inner, cross, hop, turn


def body(level_input, saved_forward, saved_reverse, filters, mixing, cotangent):
    width = level_input.shape[2]
    rows = level_input.shape[1]
    ctx = lax.axis_size(CTX)
    core = lax.axis_index("core")
    core_id = core.astype(jnp.int32).reshape(1)
    dy = cotangent[0]
    mixing = jnp.swapaxes(mixing, 0, 1)
    acc = jax.ShapeDtypeStruct((2, ROWS, width), F32)
    part = jax.ShapeDtypeStruct((rows, width), F32)
    pair = [(0, 1), (1, 0)]
    inner, cross, hop, turn = routes()
    head, tail = call(
        split_kernel,
        "split",
        tuple(jax.ShapeDtypeStruct((n, width), dy.dtype) for n in (HEAD, rows - HEAD)),
        (dy,),
        "h",
        scratch=[pltpu.SemaphoreType.DMA((2,))],
    )
    hopped = lax.ppermute(head, CTX, hop)
    crossed = lax.ppermute(tail, CTX, cross)
    left = lax.ppermute(dy, CTX, inner)
    right = lax.ppermute(dy, CTX, [(b, a) for a, b in inner])
    swap = lax.ppermute(dy, "core", pair)
    acc_near, part_near, coef, par, saved = call(
        near_kernel,
        "near",
        (
            acc,
            part,
            jax.ShapeDtypeStruct((2, COEFS, STEP // 2, width), F32),
            jax.ShapeDtypeStruct((LEVELS + 5, 2, width), F32),
            jax.ShapeDtypeStruct((2 * LEVELS - 1, rows, width), dy.dtype),
        ),
        (dy, level_input[0], saved_forward[:, 0], saved_reverse[:, 0], filters, mixing),
        "hhhhhh",
        scratch=[
            pltpu.VMEM((rows, width), dy.dtype),
            pltpu.VMEM(filters.shape, F32),
            pltpu.VMEM(mixing.shape, F32),
            pltpu.SemaphoreType.DMA((6,)),
        ],
        flops=20_000_000,
    )
    hopped, acc_near = lax.optimization_barrier((hopped, acc_near))
    turned = lax.ppermute(hopped, CTX, turn)
    left, right, turned, crossed, acc_near = lax.optimization_barrier((left, right, turned, crossed, acc_near))
    row = lax.axis_index("y")
    detour = jnp.concatenate([turned, crossed])
    left = jnp.where(row == 0, detour, left)
    right = jnp.where(row == lax.axis_size("y") - 1, detour, right)
    relay = lax.ppermute(jnp.where(core == 0, right, left), "core", pair)
    acc_far, part_far = call(
        far_kernel,
        "far",
        (acc, part),
        (core_id, swap, right, left, saved, coef, acc_near, part_near),
        "svvvvvvv",
        flops=20_000_000,
    )
    sums, grad = call(
        last_kernel,
        "last",
        (jax.ShapeDtypeStruct((8, 18 * width // LANES, LANES), F32), jax.ShapeDtypeStruct((rows, width), jnp.bfloat16)),
        (core_id, relay, saved, par, coef, acc_far, part_far),
        "svvvvvv",
        scratch=[pltpu.VMEM((2, ROWS, width), F32)],
        flops=20_000_000,
    )
    groups = (("x", "core"), ("y",), ("zl", "zh"))
    for i, axes in enumerate(groups):
        got = lax.all_to_all(sums, axes, 0, 0)
        if i + 1 < len(groups):
            sums = jnp.broadcast_to(jnp.sum(got, axis=0)[None], sums.shape)
    count = level_input.shape[0] * lax.axis_size(DP) * rows * ctx
    grad_filters, grad_mixing = call(
        lambda *refs: finish_kernel(1.0 / math.sqrt(count), *refs),
        "finish",
        (jax.ShapeDtypeStruct(filters.shape, F32), jax.ShapeDtypeStruct(mixing.shape, F32)),
        (got,),
        "v",
    )
    return grad[None], grad_filters, jnp.swapaxes(grad_mixing, 0, 1)


def solution(mesh):
    fine = Mesh(mesh.devices.reshape(4, 2, 4, 8, 2), DP + CTX)
    return jax.shard_map(
        body,
        mesh=fine,
        in_specs=(
            P(DP, CTX, None),
            P(None, DP, CTX, None),
            P(None, DP, CTX, None),
            P(),
            P(),
            P(DP, CTX, None),
        ),
        out_specs=(P(DP, CTX, None), P(), P()),
        check_vma=False,
    )
```

```python
import math

import jax
import jax.numpy as jnp
from jax import lax
from jax.experimental import pallas as pl
from jax.experimental.pallas import tpu as pltpu
from jax.sharding import Mesh
from jax.sharding import PartitionSpec as P

BLOCK = 128
NB = 8
LEVELS = 4
STEP = 16
LANES = 128
F32 = jnp.float32
DP = ("x", "zl")
CTX = ("zh", "y", "core")
SA, TA, SY, TY = 0, 1, 2, 6
SUMS = 10
ROWS = 16
F00, F01, W0, W8, C0, CD = 0, 1, 2, 3, 4, 7
COEFS = 10


def rows_of(b, n, r):
    block = n if b == 0 else NB - 1 - n
    return pl.ds(pl.multiple_of(block * BLOCK + r * STEP, STEP), STEP)


def wide(value):
    return value.astype(F32).reshape(2, STEP // 2, LANES)


def times(c, v):
    return None if v is None else c * v


def plus(*terms):
    total = None
    for term in terms:
        if term is not None:
            total = term if total is None else total + term
    return total


def share(c, dys, p):
    dy = dys.get
    sums = [None] * SUMS

    def take(row, level, n, value):
        if value is not None:
            sums[row] = plus(sums[row], p(level, n) * value)

    g = {n: plus(times(c[W0], dy(n)), times(c[W8], dy(n + 8))) for n in range(15)}
    for n in range(NB):
        take(SY + 3, 3, n, dy(n + 8))
        take(TY + 3, 3, n, dy(n))
    for level in (2, 1, 0):
        d = 2**level
        for n in range(NB):
            take(SA, level, n, g[n + d])
            take(TA, level, n, g[n])
            take(SY + level, level, n, dy(n + d))
            take(TY + level, level, n, dy(n))
        need = {2: 11, 1: 9, 0: NB}[level]
        g = {
            n: plus(
                times(c[F01], g[n]),
                times(c[F00], g[n + d]),
                times(c[C0 + level], dy(n)),
                times(c[CD + level], dy(n + d)),
            )
            for n in range(need)
        }
    return sums, g


def run(work, saved, coef_ref, acc_ref, start, finish):
    for h in range(2):
        cols = pl.ds(h * LANES, LANES)

        def step(r, accs):
            accs = list(accs)
            grads = [start(n, r, cols) for n in range(NB)]
            at = 0
            for b, sources in work:
                c = [coef_ref[b, i, :, cols][None] for i in range(COEFS)]
                dys = {}
                for ref, base in sources:
                    for j in range(NB):
                        if base + j < 23:
                            dys[base + j] = wide(ref[rows_of(b, j, r), cols])

                def p(level, n):
                    return wide(saved[3 * b + level if level else 0, rows_of(b, n, r), cols])

                sums, g = share(c, dys, p)
                for row in range(SUMS):
                    if sums[row] is not None:
                        accs[at + row] = accs[at + row] + (sums[row][0] + sums[row][1])
                at += SUMS
                for n in range(NB):
                    block = n if b == 0 else NB - 1 - n
                    grads[block] = plus(grads[block], g[n])
            for n in range(NB):
                finish(n, r, cols, grads[n].reshape(STEP, LANES))
            return tuple(accs)

        zero = jnp.zeros((STEP // 2, LANES), F32)
        accs = lax.fori_loop(0, BLOCK // STEP, step, (zero,) * (SUMS * len(work)))
        for i, (b, _) in enumerate(work):
            for row in range(SUMS):
                at = (b, pl.ds(row, 1), cols)
                acc_ref[at] = acc_ref[at] + jnp.sum(accs[i * SUMS + row], axis=0, keepdims=True)


def near_kernel(dy_hbm, first, fwd, rev, filters_hbm, mixing_hbm, acc_ref, part_ref, coef_ref, par_ref, saved, dy_ref, filters_ref, mixing_ref, sems):
    moves = [
        (filters_hbm, filters_ref),
        (mixing_hbm, mixing_ref),
        (dy_hbm, dy_ref),
        (first, saved.at[0]),
        (fwd, saved.at[pl.ds(1, LEVELS - 1)]),
        (rev, saved.at[pl.ds(LEVELS, LEVELS - 1)]),
    ]
    copies = [pltpu.make_async_copy(a, b, sems.at[i]) for i, (a, b) in enumerate(moves)]
    for copy in copies:
        copy.start()
    acc_ref[...] = jnp.zeros_like(acc_ref)
    for copy in copies[:2]:
        copy.wait()
    for b in range(2):
        f = [[filters_ref[b, i, pl.ds(j, 1), :] for j in range(2)] for i in range(2)]
        mix = [mixing_ref[i, pl.ds(b, 1), :] for i in range(LEVELS + 1)]
        c = [None] * COEFS
        c[F00], c[F01] = f[0]
        c[W0] = f[0][1] * mix[4] + f[1][1] * mix[3]
        c[W8] = f[0][0] * mix[4] + f[1][0] * mix[3]
        for level in range(3):
            c[C0 + level] = f[1][1] * mix[level]
            c[CD + level] = f[1][0] * mix[level]
        for i in range(COEFS):
            coef_ref[b, i] = jnp.broadcast_to(c[i], coef_ref.shape[2:])
        for i, value in enumerate([*f[0], *f[1], *mix]):
            par_ref[i, pl.ds(b, 1), :] = value
    for copy in copies[2:]:
        copy.wait()

    def keep(n, r, cols, value):
        part_ref[rows_of(0, n, r), cols] = value

    work = [(0, [(dy_ref, 0)]), (1, [(dy_ref, 0)])]
    run(work, saved, coef_ref, acc_ref, lambda n, r, cols: None, keep)


def pick_kernel(ids_ref, cross_ref, left_in, right_in, left_ref, right_ref, send_ref):
    core, place = ids_ref[0] % 2, ids_ref[0] // 2

    def copy(a, b):
        def step(i, carry):
            rows = pl.ds(pl.multiple_of(i * BLOCK, BLOCK), BLOCK)
            b[rows, :] = a[rows, :]
            return carry

        lax.fori_loop(0, NB, step, 0)

    pl.when(place == 0)(lambda: copy(cross_ref, left_ref))
    pl.when(place == 1)(lambda: copy(cross_ref, right_ref))
    pl.when(core == 0)(lambda: copy(right_ref, send_ref))
    pl.when(core == 1)(lambda: copy(left_ref, send_ref))


def far_kernel(ids_ref, swap_ref, right_ref, left_ref, saved, coef_ref, near_ref, part_ref, acc_ref, out_ref):
    core = ids_ref[0] % 2
    acc_ref[...] = near_ref[...]

    def start(n, r, cols):
        return part_ref[rows_of(0, n, r), cols].reshape(2, STEP // 2, LANES)

    def keep(n, r, cols, value):
        out_ref[rows_of(0, n, r), cols] = value

    for b in range(2):
        far = [[(right_ref, 2 * NB)], [(left_ref, 2 * NB)]]
        far[b] = [(swap_ref, NB)] + far[b]
        work = list(enumerate(far))
        pl.when(core == b)(lambda work=work: run(work, saved, coef_ref, acc_ref, start, keep))


def last_kernel(ids_ref, relay_ref, saved, par_ref, coef_ref, far_ref, part_ref, sums_ref, grad_ref, acc_ref):
    core = ids_ref[0] % 2
    acc_ref[...] = far_ref[...]

    def start(n, r, cols):
        return part_ref[rows_of(0, n, r), cols].reshape(2, STEP // 2, LANES)

    def keep(n, r, cols, value):
        grad_ref[rows_of(0, n, r), cols] = value.astype(grad_ref.dtype)

    for b in range(2):
        work = [(b, [(relay_ref, NB)])]
        pl.when(core == 1 - b)(
            lambda work=work: run(work, saved, coef_ref, acc_ref, start, keep)
        )
    f = [[par_ref[2 * i + j] for j in range(2)] for i in range(2)]
    mix = [par_ref[4 + i] for i in range(LEVELS + 1)]
    acc = [acc_ref[:, i, :] for i in range(SUMS)]
    s, t = acc[SY : SY + LEVELS], acc[TY : TY + LEVELS]
    sums = [
        acc[SA] + mix[4] * s[3],
        acc[TA] + mix[4] * t[3],
        sum(mix[i] * s[i] for i in range(LEVELS)),
        sum(mix[i] * t[i] for i in range(LEVELS)),
        *(f[1][0] * s[i] + f[1][1] * t[i] for i in range(LEVELS)),
        f[0][0] * s[3] + f[0][1] * t[3],
    ]
    for b in range(2):
        for j, value in enumerate(sums):
            for h in range(2):
                at = 2 * (b * 9 + j) + h
                sums_ref[0, pl.ds(at, 1), :] = value[b : b + 1, h * LANES : (h + 1) * LANES]
    for copy in range(1, sums_ref.shape[0]):
        sums_ref[copy] = sums_ref[0]


def finish_kernel(factor, got_ref, filters_ref, mixing_ref):
    total = got_ref[0]
    for i in range(1, got_ref.shape[0]):
        total = total + got_ref[i]
    total = total * factor
    for b in range(2):
        for j in range(9):
            for h in range(2):
                row = total[2 * (b * 9 + j) + h : 2 * (b * 9 + j) + h + 1]
                cols = pl.ds(h * LANES, LANES)
                if j < 4:
                    filters_ref[b, j // 2, pl.ds(j % 2, 1), cols] = row
                else:
                    mixing_ref[j - 4, pl.ds(b, 1), cols] = row


def call(kernel, name, outs, args, spaces, scratch=(), flops=0, aliases={}):
    space = {"s": pltpu.SMEM, "v": pltpu.VMEM, "h": pltpu.HBM}
    args = [pltpu.with_memory_space_constraint(a, pltpu.HBM) if k == "h" else a for a, k in zip(args, spaces)]
    return pl.pallas_call(
        kernel,
        out_shape=outs,
        in_specs=[pl.BlockSpec(memory_space=space[k]) for k in spaces],
        out_specs=(pl.BlockSpec(memory_space=pltpu.VMEM),) * len(outs),
        scratch_shapes=scratch,
        input_output_aliases=aliases,
        compiler_params=pltpu.CompilerParams(vmem_limit_bytes=8 * 1024 * 1024),
        cost_estimate=pl.CostEstimate(flops=flops, bytes_accessed=6_000_000, transcendentals=0),
        name=name,
    )(*args)


def routes():
    zs, ys, cores = (lax.axis_size(axis) for axis in CTX)

    def at(z, y, c):
        return (z * ys + y) * cores + c

    spots = [(z, c) for z in range(zs) for c in range(cores)]
    inner = [(at(z, y, c), at(z, y + 1, c)) for z, c in spots for y in range(ys - 1)]
    cross = [(at(z, ys - 1, c), at(z + 1, 0, c)) for z, c in spots if z + 1 < zs]
    return inner, cross + [(b, a) for a, b in cross]


def body(level_input, saved_forward, saved_reverse, filters, mixing, cotangent):
    width = level_input.shape[2]
    rows = level_input.shape[1]
    ctx = lax.axis_size(CTX)
    core = lax.axis_index("core")
    dy = cotangent[0]
    mixing = jnp.swapaxes(mixing, 0, 1)
    acc = jax.ShapeDtypeStruct((2, ROWS, width), F32)
    part = jax.ShapeDtypeStruct((rows, width), F32)
    pair = [(0, 1), (1, 0)]
    inner, cross = routes()
    y = lax.axis_index("y")
    place = jnp.where(y == 0, 0, jnp.where(y == lax.axis_size("y") - 1, 1, 2))
    ids = (core + 2 * place).astype(jnp.int32).reshape(1)
    ids, dy = lax.optimization_barrier((ids, dy))
    crossed = lax.ppermute(dy, CTX, cross)
    left = lax.ppermute(dy, CTX, inner)
    right = lax.ppermute(dy, CTX, [(b, a) for a, b in inner])
    swap = lax.ppermute(dy, "core", pair)
    acc_near, part_near, coef, par, saved = call(
        near_kernel,
        "near",
        (
            acc,
            part,
            jax.ShapeDtypeStruct((2, COEFS, STEP // 2, width), F32),
            jax.ShapeDtypeStruct((LEVELS + 5, 2, width), F32),
            jax.ShapeDtypeStruct((2 * LEVELS - 1, rows, width), dy.dtype),
        ),
        (dy, level_input[0], saved_forward[:, 0], saved_reverse[:, 0], filters, mixing),
        "hhhhhh",
        scratch=[
            pltpu.VMEM((rows, width), dy.dtype),
            pltpu.VMEM(filters.shape, F32),
            pltpu.VMEM(mixing.shape, F32),
            pltpu.SemaphoreType.DMA((6,)),
        ],
        flops=20_000_000,
    )
    crossed, left, right, acc_near = lax.optimization_barrier((crossed, left, right, acc_near))
    halo = jax.ShapeDtypeStruct(dy.shape, dy.dtype)
    left, right, send = call(pick_kernel, "pick", (halo,) * 3, (ids, crossed, left, right), "svvv", aliases={2: 0, 3: 1})
    relay = lax.ppermute(send, "core", pair)
    acc_far, part_far = call(
        far_kernel,
        "far",
        (acc, part),
        (ids, swap, right, left, saved, coef, acc_near, part_near),
        "svvvvvvv",
        flops=20_000_000,
    )
    sums, grad = call(
        last_kernel,
        "last",
        (jax.ShapeDtypeStruct((8, 18 * width // LANES, LANES), F32), jax.ShapeDtypeStruct((rows, width), jnp.bfloat16)),
        (ids, relay, saved, par, coef, acc_far, part_far),
        "svvvvvv",
        scratch=[pltpu.VMEM((2, ROWS, width), F32)],
        flops=20_000_000,
    )
    groups = (("x", "core"), ("y",), ("zl", "zh"))
    for i, axes in enumerate(groups):
        got = lax.all_to_all(sums, axes, 0, 0)
        if i + 1 < len(groups):
            sums = jnp.broadcast_to(jnp.sum(got, axis=0)[None], sums.shape)
    count = level_input.shape[0] * lax.axis_size(DP) * rows * ctx
    grad_filters, grad_mixing = call(
        lambda *refs: finish_kernel(1.0 / math.sqrt(count), *refs),
        "finish",
        (jax.ShapeDtypeStruct(filters.shape, F32), jax.ShapeDtypeStruct(mixing.shape, F32)),
        (got,),
        "v",
    )
    return grad[None], grad_filters, jnp.swapaxes(grad_mixing, 0, 1)


def solution(mesh):
    fine = Mesh(mesh.devices.reshape(4, 2, 4, 8, 2), DP + CTX)
    return jax.shard_map(
        body,
        mesh=fine,
        in_specs=(
            P(DP, CTX, None),
            P(None, DP, CTX, None),
            P(None, DP, CTX, None),
            P(),
            P(),
            P(DP, CTX, None),
        ),
        out_specs=(P(DP, CTX, None), P(), P()),
        check_vma=False,
    )
```

```python
import math

import jax
import jax.numpy as jnp
from jax import lax
from jax.experimental import pallas as pl
from jax.experimental.pallas import tpu as pltpu
from jax.sharding import Mesh
from jax.sharding import PartitionSpec as P

BLOCK = 128
NB = 8
LEVELS = 4
STEP = 16
LANES = 128
F32 = jnp.float32
DP = ("x", "zl")
CTX = ("zh", "y", "core")
SA, TA, SY, TY = 0, 1, 2, 6
SUMS = 10
ROWS = 16
F00, F01, W0, W8, C0, CD = 0, 1, 2, 3, 4, 7
COEFS = 10


def rows_of(b, n, r):
    block = n if b == 0 else NB - 1 - n
    return pl.ds(pl.multiple_of(block * BLOCK + r * STEP, STEP), STEP)


def wide(value):
    return value.astype(F32).reshape(2, STEP // 2, LANES)


def times(c, v):
    return None if v is None else c * v


def plus(*terms):
    total = None
    for term in terms:
        if term is not None:
            total = term if total is None else total + term
    return total


def share(c, dys, p):
    dy = dys.get
    sums = [None] * SUMS

    def take(row, level, n, value):
        if value is not None:
            sums[row] = plus(sums[row], p(level, n) * value)

    g = {n: plus(times(c[W0], dy(n)), times(c[W8], dy(n + 8))) for n in range(15)}
    for n in range(NB):
        take(SY + 3, 3, n, dy(n + 8))
        take(TY + 3, 3, n, dy(n))
    for level in (2, 1, 0):
        d = 2**level
        for n in range(NB):
            take(SA, level, n, g[n + d])
            take(TA, level, n, g[n])
            take(SY + level, level, n, dy(n + d))
            take(TY + level, level, n, dy(n))
        need = {2: 11, 1: 9, 0: NB}[level]
        g = {
            n: plus(
                times(c[F01], g[n]),
                times(c[F00], g[n + d]),
                times(c[C0 + level], dy(n)),
                times(c[CD + level], dy(n + d)),
            )
            for n in range(need)
        }
    return sums, g


def run(work, saved, coef_ref, acc_ref, start, finish, halves=(0, 1), unroll=1):
    for h in halves:
        cols = pl.ds(h * LANES, LANES)

        def step(r, accs):
            accs = list(accs)
            grads = [start(n, r, cols) for n in range(NB)]
            at = 0
            for b, sources in work:
                c = [coef_ref[b, i, :, cols][None] for i in range(COEFS)]
                dys = {}
                for ref, base in sources:
                    for j in range(NB):
                        if base + j < 23:
                            dys[base + j] = wide(ref[rows_of(b, j, r), cols])

                def p(level, n):
                    return wide(saved[3 * b + level if level else 0, rows_of(b, n, r), cols])

                sums, g = share(c, dys, p)
                for row in range(SUMS):
                    if sums[row] is not None:
                        accs[at + row] = accs[at + row] + (sums[row][0] + sums[row][1])
                at += SUMS
                for n in range(NB):
                    block = n if b == 0 else NB - 1 - n
                    grads[block] = plus(grads[block], g[n])
            for n in range(NB):
                finish(n, r, cols, grads[n].reshape(STEP, LANES))
            return tuple(accs)

        zero = jnp.zeros((STEP // 2, LANES), F32)
        accs = lax.fori_loop(0, BLOCK // STEP, step, (zero,) * (SUMS * len(work)), unroll=unroll)
        for i, (b, _) in enumerate(work):
            for row in range(SUMS):
                at = (b, pl.ds(row, 1), cols)
                acc_ref[at] = acc_ref[at] + jnp.sum(accs[i * SUMS + row], axis=0, keepdims=True)


def near_kernel(dy_hbm, first, fwd, rev, filters_hbm, mixing_hbm, acc_ref, part_ref, coef_ref, par_ref, saved, dy_ref, filters_ref, mixing_ref, sems):
    moves = [
        (filters_hbm, filters_ref),
        (mixing_hbm, mixing_ref),
        (dy_hbm, dy_ref),
        (first, saved.at[0]),
        (fwd, saved.at[pl.ds(1, LEVELS - 1)]),
        (rev, saved.at[pl.ds(LEVELS, LEVELS - 1)]),
    ]
    copies = [pltpu.make_async_copy(a, b, sems.at[i]) for i, (a, b) in enumerate(moves)]
    for copy in copies:
        copy.start()
    acc_ref[...] = jnp.zeros_like(acc_ref)
    for copy in copies[:2]:
        copy.wait()
    for b in range(2):
        f = [[filters_ref[b, i, pl.ds(j, 1), :] for j in range(2)] for i in range(2)]
        mix = [mixing_ref[i, pl.ds(b, 1), :] for i in range(LEVELS + 1)]
        c = [None] * COEFS
        c[F00], c[F01] = f[0]
        c[W0] = f[0][1] * mix[4] + f[1][1] * mix[3]
        c[W8] = f[0][0] * mix[4] + f[1][0] * mix[3]
        for level in range(3):
            c[C0 + level] = f[1][1] * mix[level]
            c[CD + level] = f[1][0] * mix[level]
        for i in range(COEFS):
            coef_ref[b, i] = jnp.broadcast_to(c[i], coef_ref.shape[2:])
        for i, value in enumerate([*f[0], *f[1], *mix]):
            par_ref[i, pl.ds(b, 1), :] = value
    for copy in copies[2:]:
        copy.wait()

    def keep(n, r, cols, value):
        part_ref[rows_of(0, n, r), cols] = value

    work = [(0, [(dy_ref, 0)]), (1, [(dy_ref, 0)])]
    run(work, saved, coef_ref, acc_ref, lambda n, r, cols: None, keep)


def pick_kernel(ids_ref, cross_ref, turn_ref, left_in, right_in, left_ref, right_ref, send_ref):
    core, detour, place = ids_ref[0] % 2, ids_ref[0] // 2 % 2, ids_ref[0] // 4

    def copy(a, b):
        def step(i, carry):
            rows = pl.ds(pl.multiple_of(i * BLOCK, BLOCK), BLOCK)
            b[rows, :] = a[rows, :]
            return carry

        lax.fori_loop(0, NB, step, 0)

    for i, to_ref in enumerate((left_ref, right_ref)):
        pl.when((place == i) & (detour == 0))(lambda to_ref=to_ref: copy(cross_ref, to_ref))
        pl.when((place == i) & (detour == 1))(lambda to_ref=to_ref: copy(turn_ref, to_ref))
    pl.when(core == 0)(lambda: copy(right_ref, send_ref))
    pl.when(core == 1)(lambda: copy(left_ref, send_ref))


def far_kernel(ids_ref, swap_ref, right_ref, left_ref, saved, coef_ref, near_ref, part_ref, acc_ref, out_ref):
    core = ids_ref[0] % 2
    acc_ref[...] = near_ref[...]

    def start(n, r, cols):
        return part_ref[rows_of(0, n, r), cols].reshape(2, STEP // 2, LANES)

    def keep(n, r, cols, value):
        out_ref[rows_of(0, n, r), cols] = value

    for b in range(2):
        far = [[(right_ref, 2 * NB)], [(left_ref, 2 * NB)]]
        far[b] = [(swap_ref, NB)] + far[b]
        work = list(enumerate(far))
        pl.when(core == b)(lambda work=work: run(work, saved, coef_ref, acc_ref, start, keep, unroll=8))


def last_kernel(ids_ref, relay_ref, saved, par_ref, coef_ref, far_ref, part_ref, sums_ref, grad_hbm, acc_ref, grad_ref, sems):
    core = ids_ref[0] % 2
    acc_ref[...] = far_ref[...]

    def start(n, r, cols):
        return part_ref[rows_of(0, n, r), cols].reshape(2, STEP // 2, LANES)

    def keep(n, r, cols, value):
        grad_ref[rows_of(0, n, r), cols] = value.astype(grad_ref.dtype)

    copies = []
    for h in range(2):
        for b in range(2):
            work = [(b, [(relay_ref, NB)])]
            pl.when(core == 1 - b)(
                lambda work=work, h=h: run(work, saved, coef_ref, acc_ref, start, keep, (h,), 8)
            )
        cols = pl.ds(h * LANES, LANES)
        copies.append(pltpu.make_async_copy(grad_ref.at[:, cols], grad_hbm.at[:, cols], sems.at[h]))
        copies[h].start()
    f = [[par_ref[2 * i + j] for j in range(2)] for i in range(2)]
    mix = [par_ref[4 + i] for i in range(LEVELS + 1)]
    acc = [acc_ref[:, i, :] for i in range(SUMS)]
    s, t = acc[SY : SY + LEVELS], acc[TY : TY + LEVELS]
    sums = [
        acc[SA] + mix[4] * s[3],
        acc[TA] + mix[4] * t[3],
        sum(mix[i] * s[i] for i in range(LEVELS)),
        sum(mix[i] * t[i] for i in range(LEVELS)),
        *(f[1][0] * s[i] + f[1][1] * t[i] for i in range(LEVELS)),
        f[0][0] * s[3] + f[0][1] * t[3],
    ]
    for b in range(2):
        for j, value in enumerate(sums):
            for h in range(2):
                at = 2 * (b * 9 + j) + h
                sums_ref[0, pl.ds(at, 1), :] = value[b : b + 1, h * LANES : (h + 1) * LANES]
    for copy in range(1, sums_ref.shape[0]):
        sums_ref[copy] = sums_ref[0]
    for copy in copies:
        copy.wait()


def finish_kernel(factor, got_ref, filters_ref, mixing_ref):
    total = got_ref[0]
    for i in range(1, got_ref.shape[0]):
        total = total + got_ref[i]
    total = total * factor
    for b in range(2):
        for j in range(9):
            for h in range(2):
                row = total[2 * (b * 9 + j) + h : 2 * (b * 9 + j) + h + 1]
                cols = pl.ds(h * LANES, LANES)
                if j < 4:
                    filters_ref[b, j // 2, pl.ds(j % 2, 1), cols] = row
                else:
                    mixing_ref[j - 4, pl.ds(b, 1), cols] = row


def call(kernel, name, outs, args, spaces, scratch=(), flops=0, aliases={}, spaces_out=None):
    space = {"s": pltpu.SMEM, "v": pltpu.VMEM, "h": pltpu.HBM, "a": pl.ANY}
    args = [pltpu.with_memory_space_constraint(a, pltpu.HBM) if k == "h" else a for a, k in zip(args, spaces)]
    return pl.pallas_call(
        kernel,
        out_shape=outs,
        in_specs=[pl.BlockSpec(memory_space=space[k]) for k in spaces],
        out_specs=tuple(pl.BlockSpec(memory_space=space[k]) for k in spaces_out or "v" * len(outs)),
        scratch_shapes=scratch,
        input_output_aliases=aliases,
        compiler_params=pltpu.CompilerParams(vmem_limit_bytes=8 * 1024 * 1024),
        cost_estimate=pl.CostEstimate(flops=flops, bytes_accessed=6_000_000, transcendentals=0),
        name=name,
    )(*args)


SEAM = ("zl",) + CTX


def routes():
    halves, zs, ys, cores = (lax.axis_size(axis) for axis in SEAM)

    def at(half, z, y, c):
        return ((half * zs + z) * ys + y) * cores + c

    spots = [(z, c) for z in range(zs) for c in range(cores)]
    inner = [(at(0, z, y, c), at(0, z, y + 1, c)) for z, c in spots for y in range(ys - 1)]
    cross, hop, turn = [], [], []
    end = ys - 1
    for half in range(halves):
        for z, c in spots:
            if z + 1 == zs:
                continue
            last, first = at(half, z, end, c), at(half, z + 1, 0, c)
            if (half, c) != (0, 1):
                cross += [(last, first), (first, last)]
                continue
            for a, middle, b in ((last, at(half, z + 1, end, c), first), (first, at(half, z, 0, c), last)):
                hop.append((a, middle))
                turn.append((middle, b))
    return inner, cross, hop, turn


def body(level_input, saved_forward, saved_reverse, filters, mixing, cotangent):
    width = level_input.shape[2]
    rows = level_input.shape[1]
    ctx = lax.axis_size(CTX)
    core = lax.axis_index("core")
    dy = cotangent[0]
    mixing = jnp.swapaxes(mixing, 0, 1)
    acc = jax.ShapeDtypeStruct((2, ROWS, width), F32)
    part = jax.ShapeDtypeStruct((rows, width), F32)
    pair = [(0, 1), (1, 0)]
    inner, cross, hop, turn = routes()
    y = lax.axis_index("y")
    place = jnp.where(y == 0, 0, jnp.where(y == lax.axis_size("y") - 1, 1, 2))
    detour = jnp.where(lax.axis_index("zl") == 0, core, 0)
    ids = (core + 2 * detour + 4 * place).astype(jnp.int32).reshape(1)
    ids, dy = lax.optimization_barrier((ids, dy))
    crossed = lax.ppermute(dy, SEAM, cross)
    hopped = lax.ppermute(dy, SEAM, hop)
    left = lax.ppermute(dy, CTX, inner)
    right = lax.ppermute(dy, CTX, [(b, a) for a, b in inner])
    swap = lax.ppermute(dy, "core", pair)
    acc_near, part_near, coef, par, saved = call(
        near_kernel,
        "near",
        (
            acc,
            part,
            jax.ShapeDtypeStruct((2, COEFS, STEP // 2, width), F32),
            jax.ShapeDtypeStruct((LEVELS + 5, 2, width), F32),
            jax.ShapeDtypeStruct((2 * LEVELS - 1, rows, width), dy.dtype),
        ),
        (dy, level_input[0], saved_forward[:, 0], saved_reverse[:, 0], filters, mixing),
        "hhhhhh",
        scratch=[
            pltpu.VMEM((rows, width), dy.dtype),
            pltpu.VMEM(filters.shape, F32),
            pltpu.VMEM(mixing.shape, F32),
            pltpu.SemaphoreType.DMA((6,)),
        ],
        flops=20_000_000,
    )
    hopped, acc_near = lax.optimization_barrier((hopped, acc_near))
    turned = lax.ppermute(hopped, SEAM, turn)
    crossed, turned, left, right = lax.optimization_barrier((crossed, turned, left, right))
    halo = jax.ShapeDtypeStruct(dy.shape, dy.dtype)
    left, right, send = call(pick_kernel, "pick", (halo,) * 3, (ids, crossed, turned, left, right), "svvvv", aliases={3: 0, 4: 1})
    relay = lax.ppermute(send, "core", pair)
    acc_far, part_far = call(
        far_kernel,
        "far",
        (acc, part),
        (ids, swap, right, left, saved, coef, acc_near, part_near),
        "svvvvvvv",
        flops=20_000_000,
    )
    sums, grad = call(
        last_kernel,
        "last",
        (jax.ShapeDtypeStruct((8, 18 * width // LANES, LANES), F32), jax.ShapeDtypeStruct((rows, width), jnp.bfloat16)),
        (ids, relay, saved, par, coef, acc_far, part_far),
        "svvvvvv",
        scratch=[
            pltpu.VMEM((2, ROWS, width), F32),
            pltpu.VMEM((rows, width), dy.dtype),
            pltpu.SemaphoreType.DMA((2,)),
        ],
        spaces_out="va",
        flops=20_000_000,
    )
    groups = (("x", "core"), ("y",), ("zl", "zh"))
    for i, axes in enumerate(groups):
        got = lax.all_to_all(sums, axes, 0, 0)
        if i + 1 < len(groups):
            sums = jnp.broadcast_to(jnp.sum(got, axis=0)[None], sums.shape)
    count = level_input.shape[0] * lax.axis_size(DP) * rows * ctx
    grad_filters, grad_mixing = call(
        lambda *refs: finish_kernel(1.0 / math.sqrt(count), *refs),
        "finish",
        (jax.ShapeDtypeStruct(filters.shape, F32), jax.ShapeDtypeStruct(mixing.shape, F32)),
        (got,),
        "v",
    )
    return grad[None], grad_filters, jnp.swapaxes(grad_mixing, 0, 1)


def solution(mesh):
    fine = Mesh(mesh.devices.reshape(4, 2, 4, 8, 2), DP + CTX)
    return jax.shard_map(
        body,
        mesh=fine,
        in_specs=(
            P(DP, CTX, None),
            P(None, DP, CTX, None),
            P(None, DP, CTX, None),
            P(),
            P(),
            P(DP, CTX, None),
        ),
        out_specs=(P(DP, CTX, None), P(), P()),
        check_vma=False,
    )
```

```python
import math

import jax
import jax.numpy as jnp
from jax import lax
from jax.experimental import pallas as pl
from jax.experimental.pallas import tpu as pltpu
from jax.sharding import Mesh
from jax.sharding import PartitionSpec as P

BLOCK = 128
NB = 8
LEVELS = 4
STEP = 16
LANES = 128
F32 = jnp.float32
DP = ("x", "zl")
CTX = ("zh", "y", "core")
SA, TA, SY, TY = 0, 1, 2, 6
SUMS = 10
ROWS = 16
F00, F01, W0, W8, C0, CD = 0, 1, 2, 3, 4, 7
COEFS = 10


def rows_of(b, n, r):
    block = n if b == 0 else NB - 1 - n
    return pl.ds(pl.multiple_of(block * BLOCK + r * STEP, STEP), STEP)


def wide(value):
    return value.astype(F32).reshape(2, STEP // 2, LANES)


def times(c, v):
    return None if v is None else c * v


def plus(*terms):
    total = None
    for term in terms:
        if term is not None:
            total = term if total is None else total + term
    return total


def share(c, dys, p):
    dy = dys.get
    sums = [None] * SUMS

    def take(row, level, n, value):
        if value is not None:
            sums[row] = plus(sums[row], p(level, n) * value)

    g = {n: plus(times(c[W0], dy(n)), times(c[W8], dy(n + 8))) for n in range(15)}
    for n in range(NB):
        take(SY + 3, 3, n, dy(n + 8))
        take(TY + 3, 3, n, dy(n))
    for level in (2, 1, 0):
        d = 2**level
        for n in range(NB):
            take(SA, level, n, g[n + d])
            take(TA, level, n, g[n])
            take(SY + level, level, n, dy(n + d))
            take(TY + level, level, n, dy(n))
        need = {2: 11, 1: 9, 0: NB}[level]
        g = {
            n: plus(
                times(c[F01], g[n]),
                times(c[F00], g[n + d]),
                times(c[C0 + level], dy(n)),
                times(c[CD + level], dy(n + d)),
            )
            for n in range(need)
        }
    return sums, g


def run(work, saved, coef_ref, acc_ref, start, finish, halves=(0, 1), unroll=1):
    for h in halves:
        cols = pl.ds(h * LANES, LANES)

        def step(r, accs):
            accs = list(accs)
            grads = [start(n, r, cols) for n in range(NB)]
            at = 0
            for b, sources in work:
                c = [coef_ref[b, i, :, cols][None] for i in range(COEFS)]
                dys = {}
                for ref, base in sources:
                    for j in range(NB):
                        if base + j < 23:
                            dys[base + j] = wide(ref[rows_of(b, j, r), cols])

                def p(level, n):
                    return wide(saved[3 * b + level if level else 0, rows_of(b, n, r), cols])

                sums, g = share(c, dys, p)
                for row in range(SUMS):
                    if sums[row] is not None:
                        accs[at + row] = accs[at + row] + (sums[row][0] + sums[row][1])
                at += SUMS
                for n in range(NB):
                    block = n if b == 0 else NB - 1 - n
                    grads[block] = plus(grads[block], g[n])
            for n in range(NB):
                finish(n, r, cols, grads[n].reshape(STEP, LANES))
            return tuple(accs)

        zero = jnp.zeros((STEP // 2, LANES), F32)
        accs = lax.fori_loop(0, BLOCK // STEP, step, (zero,) * (SUMS * len(work)), unroll=unroll)
        for i, (b, _) in enumerate(work):
            for row in range(SUMS):
                at = (b, pl.ds(row, 1), cols)
                acc_ref[at] = acc_ref[at] + jnp.sum(accs[i * SUMS + row], axis=0, keepdims=True)


def near_kernel(dy_hbm, first, fwd, rev, filters_hbm, mixing_hbm, acc_ref, part_ref, coef_ref, par_ref, saved, dy_ref, filters_ref, mixing_ref, sems):
    moves = [
        (filters_hbm, filters_ref),
        (mixing_hbm, mixing_ref),
        (dy_hbm, dy_ref),
        (first, saved.at[0]),
        (fwd, saved.at[pl.ds(1, LEVELS - 1)]),
        (rev, saved.at[pl.ds(LEVELS, LEVELS - 1)]),
    ]
    copies = [pltpu.make_async_copy(a, b, sems.at[i]) for i, (a, b) in enumerate(moves)]
    for copy in copies:
        copy.start()
    acc_ref[...] = jnp.zeros_like(acc_ref)
    for copy in copies[:2]:
        copy.wait()
    for b in range(2):
        f = [[filters_ref[b, i, pl.ds(j, 1), :] for j in range(2)] for i in range(2)]
        mix = [mixing_ref[i, pl.ds(b, 1), :] for i in range(LEVELS + 1)]
        c = [None] * COEFS
        c[F00], c[F01] = f[0]
        c[W0] = f[0][1] * mix[4] + f[1][1] * mix[3]
        c[W8] = f[0][0] * mix[4] + f[1][0] * mix[3]
        for level in range(3):
            c[C0 + level] = f[1][1] * mix[level]
            c[CD + level] = f[1][0] * mix[level]
        for i in range(COEFS):
            coef_ref[b, i] = jnp.broadcast_to(c[i], coef_ref.shape[2:])
        for i, value in enumerate([*f[0], *f[1], *mix]):
            par_ref[i, pl.ds(b, 1), :] = value
    for copy in copies[2:]:
        copy.wait()

    def keep(n, r, cols, value):
        part_ref[rows_of(0, n, r), cols] = value

    work = [(0, [(dy_ref, 0)]), (1, [(dy_ref, 0)])]
    run(work, saved, coef_ref, acc_ref, lambda n, r, cols: None, keep)


def pick_kernel(ids_ref, even_ref, odd_ref, cross_ref, turn_ref, left_ref, right_ref, send_ref):
    ids = ids_ref[0]
    core, detour, odd, place = ids % 2, ids // 2 % 2, ids // 4 % 2, ids // 8

    def copy(a, *to):
        def step(i, carry):
            rows = pl.ds(pl.multiple_of(i * BLOCK, BLOCK), BLOCK)
            value = a[rows, :]
            for b in to:
                b[rows, :] = value
            return carry

        lax.fori_loop(0, NB, step, 0)

    for side, to_ref in enumerate((left_ref, right_ref)):
        edge = place == side
        pl.when(edge & (detour == 0))(lambda to_ref=to_ref: copy(cross_ref, to_ref))
        pl.when(edge & (detour == 1))(lambda to_ref=to_ref: copy(turn_ref, to_ref))
        pl.when((place != side) & (odd != side))(lambda to_ref=to_ref: copy(even_ref, to_ref))
        pl.when((place != side) & (odd == side))(lambda to_ref=to_ref: copy(odd_ref, to_ref))
    pl.when(core == 0)(lambda: copy(right_ref, send_ref))
    pl.when(core == 1)(lambda: copy(left_ref, send_ref))


def far_kernel(ids_ref, swap_ref, right_ref, left_ref, saved, coef_ref, near_ref, part_ref, acc_ref, out_ref):
    core = ids_ref[0] % 2
    acc_ref[...] = near_ref[...]

    def start(n, r, cols):
        return part_ref[rows_of(0, n, r), cols].reshape(2, STEP // 2, LANES)

    def keep(n, r, cols, value):
        out_ref[rows_of(0, n, r), cols] = value

    for b in range(2):
        far = [[(right_ref, 2 * NB)], [(left_ref, 2 * NB)]]
        far[b] = [(swap_ref, NB)] + far[b]
        work = list(enumerate(far))
        pl.when(core == b)(lambda work=work: run(work, saved, coef_ref, acc_ref, start, keep, unroll=8))


def last_kernel(ids_ref, relay_ref, saved, par_ref, coef_ref, far_ref, part_ref, sums_ref, grad_hbm, acc_ref, grad_ref, sems):
    core = ids_ref[0] % 2
    acc_ref[...] = far_ref[...]

    def start(n, r, cols):
        return part_ref[rows_of(0, n, r), cols].reshape(2, STEP // 2, LANES)

    def keep(n, r, cols, value):
        grad_ref[rows_of(0, n, r), cols] = value.astype(grad_ref.dtype)

    copies = []
    for h in range(2):
        for b in range(2):
            work = [(b, [(relay_ref, NB)])]
            pl.when(core == 1 - b)(
                lambda work=work, h=h: run(work, saved, coef_ref, acc_ref, start, keep, (h,), 8)
            )
        cols = pl.ds(h * LANES, LANES)
        copies.append(pltpu.make_async_copy(grad_ref.at[:, cols], grad_hbm.at[:, cols], sems.at[h]))
        copies[h].start()
    f = [[par_ref[2 * i + j] for j in range(2)] for i in range(2)]
    mix = [par_ref[4 + i] for i in range(LEVELS + 1)]
    acc = [acc_ref[:, i, :] for i in range(SUMS)]
    s, t = acc[SY : SY + LEVELS], acc[TY : TY + LEVELS]
    sums = [
        acc[SA] + mix[4] * s[3],
        acc[TA] + mix[4] * t[3],
        sum(mix[i] * s[i] for i in range(LEVELS)),
        sum(mix[i] * t[i] for i in range(LEVELS)),
        *(f[1][0] * s[i] + f[1][1] * t[i] for i in range(LEVELS)),
        f[0][0] * s[3] + f[0][1] * t[3],
    ]
    for b in range(2):
        for j, value in enumerate(sums):
            for h in range(2):
                at = 2 * (b * 9 + j) + h
                sums_ref[0, pl.ds(at, 1), :] = value[b : b + 1, h * LANES : (h + 1) * LANES]
    for copy in range(1, sums_ref.shape[0]):
        sums_ref[copy] = sums_ref[0]
    for copy in copies:
        copy.wait()


def finish_kernel(factor, got_ref, filters_ref, mixing_ref):
    total = got_ref[0]
    for i in range(1, got_ref.shape[0]):
        total = total + got_ref[i]
    total = total * factor
    for b in range(2):
        for j in range(9):
            for h in range(2):
                row = total[2 * (b * 9 + j) + h : 2 * (b * 9 + j) + h + 1]
                cols = pl.ds(h * LANES, LANES)
                if j < 4:
                    filters_ref[b, j // 2, pl.ds(j % 2, 1), cols] = row
                else:
                    mixing_ref[j - 4, pl.ds(b, 1), cols] = row


def call(kernel, name, outs, args, spaces, scratch=(), flops=0, spaces_out=None):
    space = {"s": pltpu.SMEM, "v": pltpu.VMEM, "h": pltpu.HBM, "a": pl.ANY}
    args = [pltpu.with_memory_space_constraint(a, pltpu.HBM) if k == "h" else a for a, k in zip(args, spaces)]
    return pl.pallas_call(
        kernel,
        out_shape=outs,
        in_specs=[pl.BlockSpec(memory_space=space[k]) for k in spaces],
        out_specs=tuple(pl.BlockSpec(memory_space=space[k]) for k in spaces_out or "v" * len(outs)),
        scratch_shapes=scratch,
        compiler_params=pltpu.CompilerParams(vmem_limit_bytes=8 * 1024 * 1024),
        cost_estimate=pl.CostEstimate(flops=flops, bytes_accessed=6_000_000, transcendentals=0),
        name=name,
    )(*args)


SEAM = ("zl",) + CTX


def routes():
    halves, zs, ys, cores = (lax.axis_size(axis) for axis in SEAM)

    def at(half, z, y, c):
        return ((half * zs + z) * ys + y) * cores + c

    spots = [(z, c) for z in range(zs) for c in range(cores)]
    next_to = [[(at(0, z, y, c), at(0, z, y + 1, c)) for z, c in spots for y in range(odd, ys - 1, 2)] for odd in range(2)]
    even, odd = [pairs + [(b, a) for a, b in pairs] for pairs in next_to]
    cross, hop, turn = [], [], []
    end = ys - 1
    for half in range(halves):
        for z, c in spots:
            if z + 1 == zs:
                continue
            last, first = at(half, z, end, c), at(half, z + 1, 0, c)
            if (half, c) != (0, 1):
                cross += [(last, first), (first, last)]
                continue
            for a, middle, b in ((last, at(half, z + 1, end, c), first), (first, at(half, z, 0, c), last)):
                hop.append((a, middle))
                turn.append((middle, b))
    return even, odd, cross, hop, turn


def body(level_input, saved_forward, saved_reverse, filters, mixing, cotangent):
    width = level_input.shape[2]
    rows = level_input.shape[1]
    ctx = lax.axis_size(CTX)
    core = lax.axis_index("core")
    dy = cotangent[0]
    mixing = jnp.swapaxes(mixing, 0, 1)
    acc = jax.ShapeDtypeStruct((2, ROWS, width), F32)
    part = jax.ShapeDtypeStruct((rows, width), F32)
    pair = [(0, 1), (1, 0)]
    even, odd, cross, hop, turn = routes()
    y = lax.axis_index("y")
    place = jnp.where(y == 0, 0, jnp.where(y == lax.axis_size("y") - 1, 1, 2))
    detour = jnp.where(lax.axis_index("zl") == 0, core, 0)
    ids = (core + 2 * detour + 4 * (y % 2) + 8 * place).astype(jnp.int32).reshape(1)
    ids, dy = lax.optimization_barrier((ids, dy))
    crossed = lax.ppermute(dy, SEAM, cross)
    hopped = lax.ppermute(dy, SEAM, hop)
    evens = lax.ppermute(dy, CTX, even)
    odds = lax.ppermute(dy, CTX, odd)
    swap = lax.ppermute(dy, "core", pair)
    acc_near, part_near, coef, par, saved = call(
        near_kernel,
        "near",
        (
            acc,
            part,
            jax.ShapeDtypeStruct((2, COEFS, STEP // 2, width), F32),
            jax.ShapeDtypeStruct((LEVELS + 5, 2, width), F32),
            jax.ShapeDtypeStruct((2 * LEVELS - 1, rows, width), dy.dtype),
        ),
        (dy, level_input[0], saved_forward[:, 0], saved_reverse[:, 0], filters, mixing),
        "hhhhhh",
        scratch=[
            pltpu.VMEM((rows, width), dy.dtype),
            pltpu.VMEM(filters.shape, F32),
            pltpu.VMEM(mixing.shape, F32),
            pltpu.SemaphoreType.DMA((6,)),
        ],
        flops=20_000_000,
    )
    hopped, acc_near = lax.optimization_barrier((hopped, acc_near))
    turned = lax.ppermute(hopped, SEAM, turn)
    crossed, turned, evens, odds = lax.optimization_barrier((crossed, turned, evens, odds))
    halo = jax.ShapeDtypeStruct(dy.shape, dy.dtype)
    left, right, send = call(pick_kernel, "pick", (halo,) * 3, (ids, evens, odds, crossed, turned), "svvvv")
    relay = lax.ppermute(send, "core", pair)
    acc_far, part_far = call(
        far_kernel,
        "far",
        (acc, part),
        (ids, swap, right, left, saved, coef, acc_near, part_near),
        "svvvvvvv",
        flops=20_000_000,
    )
    sums, grad = call(
        last_kernel,
        "last",
        (jax.ShapeDtypeStruct((8, 18 * width // LANES, LANES), F32), jax.ShapeDtypeStruct((rows, width), jnp.bfloat16)),
        (ids, relay, saved, par, coef, acc_far, part_far),
        "svvvvvv",
        scratch=[
            pltpu.VMEM((2, ROWS, width), F32),
            pltpu.VMEM((rows, width), dy.dtype),
            pltpu.SemaphoreType.DMA((2,)),
        ],
        spaces_out="va",
        flops=20_000_000,
    )
    groups = (("x", "core"), ("y",), ("zl", "zh"))
    for i, axes in enumerate(groups):
        got = lax.all_to_all(sums, axes, 0, 0)
        if i + 1 < len(groups):
            sums = jnp.broadcast_to(jnp.sum(got, axis=0)[None], sums.shape)
    count = level_input.shape[0] * lax.axis_size(DP) * rows * ctx
    grad_filters, grad_mixing = call(
        lambda *refs: finish_kernel(1.0 / math.sqrt(count), *refs),
        "finish",
        (jax.ShapeDtypeStruct(filters.shape, F32), jax.ShapeDtypeStruct(mixing.shape, F32)),
        (got,),
        "v",
    )
    return grad[None], grad_filters, jnp.swapaxes(grad_mixing, 0, 1)


def solution(mesh):
    fine = Mesh(mesh.devices.reshape(4, 2, 4, 8, 2), DP + CTX)
    return jax.shard_map(
        body,
        mesh=fine,
        in_specs=(
            P(DP, CTX, None),
            P(None, DP, CTX, None),
            P(None, DP, CTX, None),
            P(),
            P(),
            P(DP, CTX, None),
        ),
        out_specs=(P(DP, CTX, None), P(), P()),
        check_vma=False,
    )
```

```python
import math

import jax
import jax.numpy as jnp
from jax import lax
from jax.experimental import pallas as pl
from jax.experimental.pallas import tpu as pltpu
from jax.sharding import Mesh
from jax.sharding import PartitionSpec as P

BLOCK = 128
NB = 8
LEVELS = 4
STEP = 16
LANES = 128
F32 = jnp.float32
DP = ("x", "zl")
CTX = ("zh", "y", "core")
SA, TA, SY, TY = 0, 1, 2, 6
SUMS = 10
SENT = 48
ROWS = 16
F00, F01, W0, W8, C0, CD = 0, 1, 2, 3, 4, 7
COEFS = 10


def rows_of(b, n, r):
    block = n if b == 0 else NB - 1 - n
    return pl.ds(pl.multiple_of(block * BLOCK + r * STEP, STEP), STEP)


def wide(value):
    return value.astype(F32).reshape(2, STEP // 2, LANES)


def times(c, v):
    return None if v is None else c * v


def plus(*terms):
    total = None
    for term in terms:
        if term is not None:
            total = term if total is None else total + term
    return total


def share(c, dys, p):
    dy = dys.get
    sums = [None] * SUMS

    def take(row, level, n, value):
        if value is not None:
            sums[row] = plus(sums[row], p(level, n) * value)

    g = {n: plus(times(c[W0], dy(n)), times(c[W8], dy(n + 8))) for n in range(15)}
    for n in range(NB):
        take(SY + 3, 3, n, dy(n + 8))
        take(TY + 3, 3, n, dy(n))
    for level in (2, 1, 0):
        d = 2**level
        for n in range(NB):
            take(SA, level, n, g[n + d])
            take(TA, level, n, g[n])
            take(SY + level, level, n, dy(n + d))
            take(TY + level, level, n, dy(n))
        need = {2: 11, 1: 9, 0: NB}[level]
        g = {
            n: plus(
                times(c[F01], g[n]),
                times(c[F00], g[n + d]),
                times(c[C0 + level], dy(n)),
                times(c[CD + level], dy(n + d)),
            )
            for n in range(need)
        }
    return sums, g


def run(work, saved, coef_ref, acc_ref, start, finish, halves=(0, 1), unroll=1):
    for h in halves:
        cols = pl.ds(h * LANES, LANES)

        def step(r, accs):
            accs = list(accs)
            grads = [start(n, r, cols) for n in range(NB)]
            at = 0
            for b, sources in work:
                c = [coef_ref[b, i, :, cols][None] for i in range(COEFS)]
                dys = {}
                for ref, base in sources:
                    for j in range(NB):
                        if base + j < 23:
                            dys[base + j] = wide(ref[rows_of(b, j, r), cols])

                def p(level, n):
                    return wide(saved[3 * b + level if level else 0, rows_of(b, n, r), cols])

                sums, g = share(c, dys, p)
                for row in range(SUMS):
                    if sums[row] is not None:
                        accs[at + row] = accs[at + row] + (sums[row][0] + sums[row][1])
                at += SUMS
                for n in range(NB):
                    block = n if b == 0 else NB - 1 - n
                    grads[block] = plus(grads[block], g[n])
            for n in range(NB):
                finish(n, r, cols, grads[n].reshape(STEP, LANES))
            return tuple(accs)

        zero = jnp.zeros((STEP // 2, LANES), F32)
        accs = lax.fori_loop(0, BLOCK // STEP, step, (zero,) * (SUMS * len(work)), unroll=unroll)
        for i, (b, _) in enumerate(work):
            for row in range(SUMS):
                at = (b, pl.ds(row, 1), cols)
                acc_ref[at] = acc_ref[at] + jnp.sum(accs[i * SUMS + row], axis=0, keepdims=True)


def near_kernel(dy_hbm, first, fwd, rev, filters_hbm, mixing_hbm, acc_ref, part_ref, coef_ref, par_ref, saved, dy_ref, filters_ref, mixing_ref, sems):
    moves = [
        (filters_hbm, filters_ref),
        (mixing_hbm, mixing_ref),
        (dy_hbm, dy_ref),
        (first, saved.at[0]),
        (fwd, saved.at[pl.ds(1, LEVELS - 1)]),
        (rev, saved.at[pl.ds(LEVELS, LEVELS - 1)]),
    ]
    copies = [pltpu.make_async_copy(a, b, sems.at[i]) for i, (a, b) in enumerate(moves)]
    for copy in copies:
        copy.start()
    acc_ref[...] = jnp.zeros_like(acc_ref)
    for copy in copies[:2]:
        copy.wait()
    for b in range(2):
        f = [[filters_ref[b, i, pl.ds(j, 1), :] for j in range(2)] for i in range(2)]
        mix = [mixing_ref[i, pl.ds(b, 1), :] for i in range(LEVELS + 1)]
        c = [None] * COEFS
        c[F00], c[F01] = f[0]
        c[W0] = f[0][1] * mix[4] + f[1][1] * mix[3]
        c[W8] = f[0][0] * mix[4] + f[1][0] * mix[3]
        for level in range(3):
            c[C0 + level] = f[1][1] * mix[level]
            c[CD + level] = f[1][0] * mix[level]
        for i in range(COEFS):
            coef_ref[b, i] = jnp.broadcast_to(c[i], coef_ref.shape[2:])
        for i, value in enumerate([*f[0], *f[1], *mix]):
            par_ref[i, pl.ds(b, 1), :] = value
    for copy in copies[2:]:
        copy.wait()

    def keep(n, r, cols, value):
        part_ref[rows_of(0, n, r), cols] = value

    work = [(0, [(dy_ref, 0)]), (1, [(dy_ref, 0)])]
    run(work, saved, coef_ref, acc_ref, lambda n, r, cols: None, keep)


def pick_kernel(ids_ref, even_ref, odd_ref, cross_ref, turn_ref, left_ref, right_ref, send_ref):
    ids = ids_ref[0]
    core, detour, odd, place = ids % 2, ids // 2 % 2, ids // 4 % 2, ids // 8

    def copy(a, *to):
        def step(i, carry):
            rows = pl.ds(pl.multiple_of(i * BLOCK, BLOCK), BLOCK)
            value = a[rows, :]
            for b in to:
                b[rows, :] = value
            return carry

        lax.fori_loop(0, NB, step, 0)

    for side, to_ref in enumerate((left_ref, right_ref)):
        edge = place == side
        pl.when(edge & (detour == 0))(lambda to_ref=to_ref: copy(cross_ref, to_ref))
        pl.when(edge & (detour == 1))(lambda to_ref=to_ref: copy(turn_ref, to_ref))
        pl.when((place != side) & (odd != side))(lambda to_ref=to_ref: copy(even_ref, to_ref))
        pl.when((place != side) & (odd == side))(lambda to_ref=to_ref: copy(odd_ref, to_ref))
    pl.when(core == 0)(lambda: copy(right_ref, send_ref))
    pl.when(core == 1)(lambda: copy(left_ref, send_ref))


def far_kernel(ids_ref, swap_ref, right_ref, left_ref, saved, coef_ref, near_ref, part_ref, acc_ref, out_ref):
    core = ids_ref[0] % 2
    acc_ref[...] = near_ref[...]

    def start(n, r, cols):
        return part_ref[rows_of(0, n, r), cols].reshape(2, STEP // 2, LANES)

    def keep(n, r, cols, value):
        out_ref[rows_of(0, n, r), cols] = value

    for b in range(2):
        far = [[(right_ref, 2 * NB)], [(left_ref, 2 * NB)]]
        far[b] = [(swap_ref, NB)] + far[b]
        work = list(enumerate(far))
        pl.when(core == b)(lambda work=work: run(work, saved, coef_ref, acc_ref, start, keep, unroll=8))


def last_kernel(ids_ref, relay_ref, saved, par_ref, coef_ref, far_ref, part_ref, sums_ref, grad_hbm, acc_ref, sum_ref, grad_ref, sems):
    core = ids_ref[0] % 2
    acc_ref[...] = far_ref[...]
    sum_ref[...] = jnp.zeros_like(sum_ref)

    def start(n, r, cols):
        return part_ref[rows_of(0, n, r), cols].reshape(2, STEP // 2, LANES)

    def keep(n, r, cols, value):
        grad_ref[rows_of(0, n, r), cols] = value.astype(grad_ref.dtype)

    copies = []
    for h in range(2):
        for b in range(2):
            work = [(b, [(relay_ref, NB)])]
            pl.when(core == 1 - b)(
                lambda work=work, h=h: run(work, saved, coef_ref, acc_ref, start, keep, (h,), 8)
            )
        cols = pl.ds(h * LANES, LANES)
        copies.append(pltpu.make_async_copy(grad_ref.at[:, cols], grad_hbm.at[:, cols], sems.at[h]))
        copies[h].start()
    f = [[par_ref[2 * i + j] for j in range(2)] for i in range(2)]
    mix = [par_ref[4 + i] for i in range(LEVELS + 1)]
    acc = [acc_ref[:, i, :] for i in range(SUMS)]
    s, t = acc[SY : SY + LEVELS], acc[TY : TY + LEVELS]
    sums = [
        acc[SA] + mix[4] * s[3],
        acc[TA] + mix[4] * t[3],
        sum(mix[i] * s[i] for i in range(LEVELS)),
        sum(mix[i] * t[i] for i in range(LEVELS)),
        *(f[1][0] * s[i] + f[1][1] * t[i] for i in range(LEVELS)),
        f[0][0] * s[3] + f[0][1] * t[3],
    ]
    for b in range(2):
        for j, value in enumerate(sums):
            for h in range(2):
                at = 2 * (b * 9 + j) + h
                sum_ref[pl.ds(at, 1), :] = value[b : b + 1, h * LANES : (h + 1) * LANES]
    sent = sum_ref[...].astype(sums_ref.dtype)
    for copy in range(sums_ref.shape[0]):
        sums_ref[copy] = sent
    for copy in copies:
        copy.wait()


def total_of(got_ref):
    total = got_ref[0].astype(F32)
    for i in range(1, got_ref.shape[0]):
        total = total + got_ref[i].astype(F32)
    return total


def fold_kernel(got_ref, sums_ref):
    total = total_of(got_ref).astype(sums_ref.dtype)
    for copy in range(sums_ref.shape[0]):
        sums_ref[copy] = total


def finish_kernel(factor, got_ref, filters_ref, mixing_ref):
    total = total_of(got_ref) * factor
    for b in range(2):
        for j in range(9):
            for h in range(2):
                row = total[2 * (b * 9 + j) + h : 2 * (b * 9 + j) + h + 1]
                cols = pl.ds(h * LANES, LANES)
                if j < 4:
                    filters_ref[b, j // 2, pl.ds(j % 2, 1), cols] = row
                else:
                    mixing_ref[j - 4, pl.ds(b, 1), cols] = row


def call(kernel, name, outs, args, spaces, scratch=(), flops=0, spaces_out=None):
    space = {"s": pltpu.SMEM, "v": pltpu.VMEM, "h": pltpu.HBM, "a": pl.ANY}
    args = [pltpu.with_memory_space_constraint(a, pltpu.HBM) if k == "h" else a for a, k in zip(args, spaces)]
    return pl.pallas_call(
        kernel,
        out_shape=outs,
        in_specs=[pl.BlockSpec(memory_space=space[k]) for k in spaces],
        out_specs=tuple(pl.BlockSpec(memory_space=space[k]) for k in spaces_out or "v" * len(outs)),
        scratch_shapes=scratch,
        compiler_params=pltpu.CompilerParams(vmem_limit_bytes=8 * 1024 * 1024),
        cost_estimate=pl.CostEstimate(flops=flops, bytes_accessed=6_000_000, transcendentals=0),
        name=name,
    )(*args)


SEAM = ("zl",) + CTX


def routes():
    halves, zs, ys, cores = (lax.axis_size(axis) for axis in SEAM)

    def at(half, z, y, c):
        return ((half * zs + z) * ys + y) * cores + c

    spots = [(z, c) for z in range(zs) for c in range(cores)]
    next_to = [[(at(0, z, y, c), at(0, z, y + 1, c)) for z, c in spots for y in range(odd, ys - 1, 2)] for odd in range(2)]
    even, odd = [pairs + [(b, a) for a, b in pairs] for pairs in next_to]
    cross, hop, turn = [], [], []
    end = ys - 1
    for half in range(halves):
        for z, c in spots:
            if z + 1 == zs:
                continue
            last, first = at(half, z, end, c), at(half, z + 1, 0, c)
            if (half, c) != (0, 1):
                cross += [(last, first), (first, last)]
                continue
            for a, middle, b in ((last, at(half, z + 1, end, c), first), (first, at(half, z, 0, c), last)):
                hop.append((a, middle))
                turn.append((middle, b))
    return even, odd, cross, hop, turn


def body(level_input, saved_forward, saved_reverse, filters, mixing, cotangent):
    width = level_input.shape[2]
    rows = level_input.shape[1]
    ctx = lax.axis_size(CTX)
    core = lax.axis_index("core")
    dy = cotangent[0]
    mixing = jnp.swapaxes(mixing, 0, 1)
    acc = jax.ShapeDtypeStruct((2, ROWS, width), F32)
    part = jax.ShapeDtypeStruct((rows, width), F32)
    pair = [(0, 1), (1, 0)]
    even, odd, cross, hop, turn = routes()
    y = lax.axis_index("y")
    place = jnp.where(y == 0, 0, jnp.where(y == lax.axis_size("y") - 1, 1, 2))
    detour = jnp.where(lax.axis_index("zl") == 0, core, 0)
    ids = (core + 2 * detour + 4 * (y % 2) + 8 * place).astype(jnp.int32).reshape(1)
    ids, dy = lax.optimization_barrier((ids, dy))
    crossed = lax.ppermute(dy, SEAM, cross)
    hopped = lax.ppermute(dy, SEAM, hop)
    evens = lax.ppermute(dy, CTX, even)
    odds = lax.ppermute(dy, CTX, odd)
    swap = lax.ppermute(dy, "core", pair)
    acc_near, part_near, coef, par, saved = call(
        near_kernel,
        "near",
        (
            acc,
            part,
            jax.ShapeDtypeStruct((2, COEFS, STEP // 2, width), F32),
            jax.ShapeDtypeStruct((LEVELS + 5, 2, width), F32),
            jax.ShapeDtypeStruct((2 * LEVELS - 1, rows, width), dy.dtype),
        ),
        (dy, level_input[0], saved_forward[:, 0], saved_reverse[:, 0], filters, mixing),
        "hhhhhh",
        scratch=[
            pltpu.VMEM((rows, width), dy.dtype),
            pltpu.VMEM(filters.shape, F32),
            pltpu.VMEM(mixing.shape, F32),
            pltpu.SemaphoreType.DMA((6,)),
        ],
        flops=20_000_000,
    )
    hopped, acc_near = lax.optimization_barrier((hopped, acc_near))
    turned = lax.ppermute(hopped, SEAM, turn)
    crossed, turned, evens, odds = lax.optimization_barrier((crossed, turned, evens, odds))
    halo = jax.ShapeDtypeStruct(dy.shape, dy.dtype)
    left, right, send = call(pick_kernel, "pick", (halo,) * 3, (ids, evens, odds, crossed, turned), "svvvv")
    relay = lax.ppermute(send, "core", pair)
    acc_far, part_far = call(
        far_kernel,
        "far",
        (acc, part),
        (ids, swap, right, left, saved, coef, acc_near, part_near),
        "svvvvvvv",
        flops=20_000_000,
    )
    sums, grad = call(
        last_kernel,
        "last",
        (jax.ShapeDtypeStruct((8, SENT, LANES), dy.dtype), jax.ShapeDtypeStruct((rows, width), jnp.bfloat16)),
        (ids, relay, saved, par, coef, acc_far, part_far),
        "svvvvvv",
        scratch=[
            pltpu.VMEM((2, ROWS, width), F32),
            pltpu.VMEM((SENT, LANES), F32),
            pltpu.VMEM((rows, width), dy.dtype),
            pltpu.SemaphoreType.DMA((2,)),
        ],
        spaces_out="va",
        flops=20_000_000,
    )
    groups = (("x", "core"), ("y",), ("zl", "zh"))
    for i, axes in enumerate(groups):
        got = lax.all_to_all(sums, axes, 0, 0)
        if i + 1 < len(groups):
            (sums,) = call(fold_kernel, "fold", (jax.ShapeDtypeStruct(sums.shape, sums.dtype),), (got,), "v")
    count = level_input.shape[0] * lax.axis_size(DP) * rows * ctx
    grad_filters, grad_mixing = call(
        lambda *refs: finish_kernel(1.0 / math.sqrt(count), *refs),
        "finish",
        (jax.ShapeDtypeStruct(filters.shape, F32), jax.ShapeDtypeStruct(mixing.shape, F32)),
        (got,),
        "v",
    )
    return grad[None], grad_filters, jnp.swapaxes(grad_mixing, 0, 1)


def solution(mesh):
    fine = Mesh(mesh.devices.reshape(4, 2, 4, 8, 2), DP + CTX)
    return jax.shard_map(
        body,
        mesh=fine,
        in_specs=(
            P(DP, CTX, None),
            P(None, DP, CTX, None),
            P(None, DP, CTX, None),
            P(),
            P(),
            P(DP, CTX, None),
        ),
        out_specs=(P(DP, CTX, None), P(), P()),
        check_vma=False,
    )
```

```python
import math

import jax
import jax.numpy as jnp
from jax import lax
from jax.experimental import pallas as pl
from jax.experimental.pallas import tpu as pltpu
from jax.sharding import Mesh
from jax.sharding import PartitionSpec as P

BLOCK = 128
NB = 8
LEVELS = 4
STEP = 16
LANES = 128
F32 = jnp.float32
DP = ("x", "zl")
CTX = ("zh", "y", "core")
SA, TA, SY, TY = 0, 1, 2, 6
SUMS = 10
SENT = 48
ROWS = 16
F00, F01, W0, W8, C0, CD = 0, 1, 2, 3, 4, 7
COEFS = 10


def rows_of(b, n, r):
    block = n if b == 0 else NB - 1 - n
    return pl.ds(pl.multiple_of(block * BLOCK + r * STEP, STEP), STEP)


def wide(value):
    return value.astype(F32).reshape(2, STEP // 2, LANES)


def times(c, v):
    return None if v is None else c * v


def plus(*terms):
    total = None
    for term in terms:
        if term is not None:
            total = term if total is None else total + term
    return total


def share(c, dys, p):
    dy = dys.get
    sums = [None] * SUMS

    def take(row, level, n, value):
        if value is not None:
            sums[row] = plus(sums[row], p(level, n) * value)

    g = {n: plus(times(c[W0], dy(n)), times(c[W8], dy(n + 8))) for n in range(15)}
    for n in range(NB):
        take(SY + 3, 3, n, dy(n + 8))
        take(TY + 3, 3, n, dy(n))
    for level in (2, 1, 0):
        d = 2**level
        for n in range(NB):
            take(SA, level, n, g[n + d])
            take(TA, level, n, g[n])
            take(SY + level, level, n, dy(n + d))
            take(TY + level, level, n, dy(n))
        need = {2: 11, 1: 9, 0: NB}[level]
        g = {
            n: plus(
                times(c[F01], g[n]),
                times(c[F00], g[n + d]),
                times(c[C0 + level], dy(n)),
                times(c[CD + level], dy(n + d)),
            )
            for n in range(need)
        }
    return sums, g


def run(work, saved, coef_ref, acc_ref, start, finish, unroll=1):
    for h in range(2):
        cols = pl.ds(h * LANES, LANES)

        def step(r, accs):
            accs = list(accs)
            grads = [start(n, r, cols) for n in range(NB)]
            at = 0
            for b, sources in work:
                c = [coef_ref[b, i, :, cols][None] for i in range(COEFS)]
                dys = {}
                for ref, base in sources:
                    for j in range(NB):
                        if base + j < 23:
                            dys[base + j] = wide(ref[rows_of(b, j, r), cols])

                def p(level, n):
                    return wide(saved[3 * b + level if level else 0, rows_of(b, n, r), cols])

                sums, g = share(c, dys, p)
                for row in range(SUMS):
                    if sums[row] is not None:
                        accs[at + row] = accs[at + row] + (sums[row][0] + sums[row][1])
                at += SUMS
                for n in range(NB):
                    block = n if b == 0 else NB - 1 - n
                    grads[block] = plus(grads[block], g[n])
            for n in range(NB):
                finish(n, r, cols, grads[n].reshape(STEP, LANES))
            return tuple(accs)

        zero = jnp.zeros((STEP // 2, LANES), F32)
        accs = lax.fori_loop(0, BLOCK // STEP, step, (zero,) * (SUMS * len(work)), unroll=unroll)
        for i, (b, _) in enumerate(work):
            for row in range(SUMS):
                at = (b, pl.ds(row, 1), cols)
                acc_ref[at] = acc_ref[at] + jnp.sum(accs[i * SUMS + row], axis=0, keepdims=True)


def near_kernel(dy_hbm, first, fwd, rev, filters_hbm, mixing_hbm, acc_ref, part_ref, coef_ref, par_ref, saved, dy_ref, filters_ref, mixing_ref, sems):
    moves = [
        (filters_hbm, filters_ref),
        (mixing_hbm, mixing_ref),
        (dy_hbm, dy_ref),
        (first, saved.at[0]),
        (fwd, saved.at[pl.ds(1, LEVELS - 1)]),
        (rev, saved.at[pl.ds(LEVELS, LEVELS - 1)]),
    ]
    copies = [pltpu.make_async_copy(a, b, sems.at[i]) for i, (a, b) in enumerate(moves)]
    for copy in copies:
        copy.start()
    acc_ref[...] = jnp.zeros_like(acc_ref)
    for copy in copies[:2]:
        copy.wait()
    for b in range(2):
        f = [[filters_ref[b, i, pl.ds(j, 1), :] for j in range(2)] for i in range(2)]
        mix = [mixing_ref[i, pl.ds(b, 1), :] for i in range(LEVELS + 1)]
        c = [None] * COEFS
        c[F00], c[F01] = f[0]
        c[W0] = f[0][1] * mix[4] + f[1][1] * mix[3]
        c[W8] = f[0][0] * mix[4] + f[1][0] * mix[3]
        for level in range(3):
            c[C0 + level] = f[1][1] * mix[level]
            c[CD + level] = f[1][0] * mix[level]
        for i in range(COEFS):
            coef_ref[b, i] = jnp.broadcast_to(c[i], coef_ref.shape[2:])
        for i, value in enumerate([*f[0], *f[1], *mix]):
            par_ref[i, pl.ds(b, 1), :] = value
    for copy in copies[2:]:
        copy.wait()

    def keep(n, r, cols, value):
        part_ref[rows_of(0, n, r), cols] = value

    work = [(0, [(dy_ref, 0)]), (1, [(dy_ref, 0)])]
    run(work, saved, coef_ref, acc_ref, lambda n, r, cols: None, keep)


def pick_kernel(ids_ref, even_ref, odd_ref, cross_ref, turn_ref, left_ref, right_ref, send_ref):
    ids = ids_ref[0]
    core, detour, odd, place = ids % 2, ids // 2 % 2, ids // 4 % 2, ids // 8

    def copy(a, *to):
        def step(i, carry):
            rows = pl.ds(pl.multiple_of(i * BLOCK, BLOCK), BLOCK)
            value = a[rows, :]
            for b in to:
                b[rows, :] = value
            return carry

        lax.fori_loop(0, NB, step, 0)

    for side, to_ref in enumerate((left_ref, right_ref)):
        edge = place == side
        pl.when(edge & (detour == 0))(lambda to_ref=to_ref: copy(cross_ref, to_ref))
        pl.when(edge & (detour == 1))(lambda to_ref=to_ref: copy(turn_ref, to_ref))
        pl.when((place != side) & (odd != side))(lambda to_ref=to_ref: copy(even_ref, to_ref))
        pl.when((place != side) & (odd == side))(lambda to_ref=to_ref: copy(odd_ref, to_ref))
    pl.when(core == 0)(lambda: copy(right_ref, send_ref))
    pl.when(core == 1)(lambda: copy(left_ref, send_ref))


def far_kernel(ids_ref, swap_ref, right_ref, left_ref, saved, coef_ref, near_ref, part_ref, acc_ref, out_ref):
    core = ids_ref[0] % 2
    acc_ref[...] = near_ref[...]

    def start(n, r, cols):
        return part_ref[rows_of(0, n, r), cols].reshape(2, STEP // 2, LANES)

    def keep(n, r, cols, value):
        out_ref[rows_of(0, n, r), cols] = value

    for b in range(2):
        far = [[(right_ref, 2 * NB)], [(left_ref, 2 * NB)]]
        far[b] = [(swap_ref, NB)] + far[b]
        work = list(enumerate(far))
        pl.when(core == b)(lambda work=work: run(work, saved, coef_ref, acc_ref, start, keep, unroll=8))


def last_kernel(ids_ref, relay_ref, saved, par_ref, coef_ref, far_ref, part_ref, sums_ref, grad_ref, acc_ref, sum_ref):
    core = ids_ref[0] % 2
    acc_ref[...] = far_ref[...]
    sum_ref[...] = jnp.zeros_like(sum_ref)

    def start(n, r, cols):
        return part_ref[rows_of(0, n, r), cols].reshape(2, STEP // 2, LANES)

    def keep(n, r, cols, value):
        grad_ref[rows_of(0, n, r), cols] = value.astype(grad_ref.dtype)

    for b in range(2):
        work = [(b, [(relay_ref, NB)])]
        pl.when(core == 1 - b)(
            lambda work=work: run(work, saved, coef_ref, acc_ref, start, keep, unroll=8)
        )
    f = [[par_ref[2 * i + j] for j in range(2)] for i in range(2)]
    mix = [par_ref[4 + i] for i in range(LEVELS + 1)]
    acc = [acc_ref[:, i, :] for i in range(SUMS)]
    s, t = acc[SY : SY + LEVELS], acc[TY : TY + LEVELS]
    sums = [
        acc[SA] + mix[4] * s[3],
        acc[TA] + mix[4] * t[3],
        sum(mix[i] * s[i] for i in range(LEVELS)),
        sum(mix[i] * t[i] for i in range(LEVELS)),
        *(f[1][0] * s[i] + f[1][1] * t[i] for i in range(LEVELS)),
        f[0][0] * s[3] + f[0][1] * t[3],
    ]
    for b in range(2):
        for j, value in enumerate(sums):
            for h in range(2):
                at = 2 * (b * 9 + j) + h
                sum_ref[pl.ds(at, 1), :] = value[b : b + 1, h * LANES : (h + 1) * LANES]
    sent = sum_ref[...].astype(sums_ref.dtype)
    for copy in range(sums_ref.shape[0]):
        sums_ref[copy] = sent


def total_of(got_ref):
    total = got_ref[0].astype(F32)
    for i in range(1, got_ref.shape[0]):
        total = total + got_ref[i].astype(F32)
    return total


def fold_kernel(got_ref, sums_ref):
    total = total_of(got_ref).astype(sums_ref.dtype)
    for copy in range(sums_ref.shape[0]):
        sums_ref[copy] = total


def finish_kernel(factor, got_ref, grad_ref, filters_hbm, mixing_hbm, grad_hbm, filters_ref, mixing_ref, sems):
    moves = ((grad_ref, grad_hbm), (filters_ref, filters_hbm), (mixing_ref, mixing_hbm))
    copies = [pltpu.make_async_copy(a, b, sems.at[i]) for i, (a, b) in enumerate(moves)]
    copies[0].start()
    total = total_of(got_ref) * factor
    for b in range(2):
        for j in range(9):
            for h in range(2):
                row = total[2 * (b * 9 + j) + h : 2 * (b * 9 + j) + h + 1]
                cols = pl.ds(h * LANES, LANES)
                if j < 4:
                    filters_ref[b, j // 2, pl.ds(j % 2, 1), cols] = row
                else:
                    mixing_ref[j - 4, pl.ds(b, 1), cols] = row
    for copy in copies[1:]:
        copy.start()
    for copy in copies:
        copy.wait()


def call(kernel, name, outs, args, spaces, scratch=(), flops=0, spaces_out=None):
    space = {"s": pltpu.SMEM, "v": pltpu.VMEM, "h": pltpu.HBM, "a": pl.ANY}
    args = [pltpu.with_memory_space_constraint(a, pltpu.HBM) if k == "h" else a for a, k in zip(args, spaces)]
    return pl.pallas_call(
        kernel,
        out_shape=outs,
        in_specs=[pl.BlockSpec(memory_space=space[k]) for k in spaces],
        out_specs=tuple(pl.BlockSpec(memory_space=space[k]) for k in spaces_out or "v" * len(outs)),
        scratch_shapes=scratch,
        compiler_params=pltpu.CompilerParams(vmem_limit_bytes=8 * 1024 * 1024),
        cost_estimate=pl.CostEstimate(flops=flops, bytes_accessed=6_000_000, transcendentals=0),
        name=name,
    )(*args)


SEAM = ("zl",) + CTX


def routes():
    halves, zs, ys, cores = (lax.axis_size(axis) for axis in SEAM)

    def at(half, z, y, c):
        return ((half * zs + z) * ys + y) * cores + c

    spots = [(z, c) for z in range(zs) for c in range(cores)]
    next_to = [[(at(0, z, y, c), at(0, z, y + 1, c)) for z, c in spots for y in range(odd, ys - 1, 2)] for odd in range(2)]
    even, odd = [pairs + [(b, a) for a, b in pairs] for pairs in next_to]
    cross, hop, turn = [], [], []
    end = ys - 1
    for half in range(halves):
        for z, c in spots:
            if z + 1 == zs:
                continue
            last, first = at(half, z, end, c), at(half, z + 1, 0, c)
            if (half, c) != (0, 1):
                cross += [(last, first), (first, last)]
                continue
            for a, middle, b in ((last, at(half, z + 1, end, c), first), (first, at(half, z, 0, c), last)):
                hop.append((a, middle))
                turn.append((middle, b))
    return even, odd, cross, hop, turn


def body(level_input, saved_forward, saved_reverse, filters, mixing, cotangent):
    width = level_input.shape[2]
    rows = level_input.shape[1]
    ctx = lax.axis_size(CTX)
    core = lax.axis_index("core")
    dy = cotangent[0]
    mixing = jnp.swapaxes(mixing, 0, 1)
    acc = jax.ShapeDtypeStruct((2, ROWS, width), F32)
    part = jax.ShapeDtypeStruct((rows, width), F32)
    pair = [(0, 1), (1, 0)]
    even, odd, cross, hop, turn = routes()
    y = lax.axis_index("y")
    place = jnp.where(y == 0, 0, jnp.where(y == lax.axis_size("y") - 1, 1, 2))
    detour = jnp.where(lax.axis_index("zl") == 0, core, 0)
    ids = (core + 2 * detour + 4 * (y % 2) + 8 * place).astype(jnp.int32).reshape(1)
    ids, dy = lax.optimization_barrier((ids, dy))
    crossed = lax.ppermute(dy, SEAM, cross)
    hopped = lax.ppermute(dy, SEAM, hop)
    evens = lax.ppermute(dy, CTX, even)
    odds = lax.ppermute(dy, CTX, odd)
    swap = lax.ppermute(dy, "core", pair)
    acc_near, part_near, coef, par, saved = call(
        near_kernel,
        "near",
        (
            acc,
            part,
            jax.ShapeDtypeStruct((2, COEFS, STEP // 2, width), F32),
            jax.ShapeDtypeStruct((LEVELS + 5, 2, width), F32),
            jax.ShapeDtypeStruct((2 * LEVELS - 1, rows, width), dy.dtype),
        ),
        (dy, level_input[0], saved_forward[:, 0], saved_reverse[:, 0], filters, mixing),
        "hhhhhh",
        scratch=[
            pltpu.VMEM((rows, width), dy.dtype),
            pltpu.VMEM(filters.shape, F32),
            pltpu.VMEM(mixing.shape, F32),
            pltpu.SemaphoreType.DMA((6,)),
        ],
        flops=20_000_000,
    )
    hopped, acc_near = lax.optimization_barrier((hopped, acc_near))
    turned = lax.ppermute(hopped, SEAM, turn)
    crossed, turned, evens, odds = lax.optimization_barrier((crossed, turned, evens, odds))
    halo = jax.ShapeDtypeStruct(dy.shape, dy.dtype)
    left, right, send = call(pick_kernel, "pick", (halo,) * 3, (ids, evens, odds, crossed, turned), "svvvv")
    relay = lax.ppermute(send, "core", pair)
    acc_far, part_far = call(
        far_kernel,
        "far",
        (acc, part),
        (ids, swap, right, left, saved, coef, acc_near, part_near),
        "svvvvvvv",
        flops=20_000_000,
    )
    sums, grad = call(
        last_kernel,
        "last",
        (jax.ShapeDtypeStruct((8, SENT, LANES), dy.dtype), pltpu.VMEM((rows, width), jnp.bfloat16)),
        (ids, relay, saved, par, coef, acc_far, part_far),
        "svvvvvv",
        scratch=[
            pltpu.VMEM((2, ROWS, width), F32),
            pltpu.VMEM((SENT, LANES), F32),
        ],
        flops=20_000_000,
    )
    groups = (("x", "core"), ("y",), ("zl", "zh"))
    for i, axes in enumerate(groups):
        got = lax.all_to_all(sums, axes, 0, 0)
        if i + 1 < len(groups):
            (sums,) = call(fold_kernel, "fold", (jax.ShapeDtypeStruct(sums.shape, sums.dtype),), (got,), "v")
    count = level_input.shape[0] * lax.axis_size(DP) * rows * ctx
    grad_filters, grad_mixing, grad = call(
        lambda *refs: finish_kernel(1.0 / math.sqrt(count), *refs),
        "finish",
        (jax.ShapeDtypeStruct(filters.shape, F32), jax.ShapeDtypeStruct(mixing.shape, F32), jax.ShapeDtypeStruct(grad.shape, grad.dtype)),
        (got, grad),
        "vv",
        scratch=[
            pltpu.VMEM(filters.shape, F32),
            pltpu.VMEM(mixing.shape, F32),
            pltpu.SemaphoreType.DMA((3,)),
        ],
        spaces_out="aaa",
    )
    return grad[None], grad_filters, jnp.swapaxes(grad_mixing, 0, 1)


def solution(mesh):
    fine = Mesh(mesh.devices.reshape(4, 2, 4, 8, 2), DP + CTX)
    return jax.shard_map(
        body,
        mesh=fine,
        in_specs=(
            P(DP, CTX, None),
            P(None, DP, CTX, None),
            P(None, DP, CTX, None),
            P(),
            P(),
            P(DP, CTX, None),
        ),
        out_specs=(P(DP, CTX, None), P(), P()),
        check_vma=False,
    )
```

```python
import math

import jax
import jax.numpy as jnp
from jax import lax
from jax.experimental import pallas as pl
from jax.experimental.pallas import tpu as pltpu
from jax.sharding import Mesh
from jax.sharding import PartitionSpec as P

BLOCK = 128
NB = 8
LEVELS = 4
STEP = 16
LANES = 128
F32 = jnp.float32
DP = ("x", "zl")
CTX = ("zh", "y", "core")
SA, TA, SY, TY = 0, 1, 2, 6
SUMS = 10
SENT = 40
ROWS = 16
F00, F01, W0, W8, C0, CD = 0, 1, 2, 3, 4, 7
COEFS = 10


def rows_of(b, n, r):
    block = n if b == 0 else NB - 1 - n
    return pl.ds(pl.multiple_of(block * BLOCK + r * STEP, STEP), STEP)


def wide(value):
    return value.astype(F32).reshape(2, STEP // 2, LANES)


def times(c, v):
    return None if v is None else c * v


def plus(*terms):
    total = None
    for term in terms:
        if term is not None:
            total = term if total is None else total + term
    return total


def share(c, dys, p):
    dy = dys.get
    sums = [None] * SUMS

    def take(row, level, n, value):
        if value is not None:
            sums[row] = plus(sums[row], p(level, n) * value)

    g = {n: plus(times(c[W0], dy(n)), times(c[W8], dy(n + 8))) for n in range(15)}
    for n in range(NB):
        take(SY + 3, 3, n, dy(n + 8))
        take(TY + 3, 3, n, dy(n))
    for level in (2, 1, 0):
        d = 2**level
        for n in range(NB):
            take(SA, level, n, g[n + d])
            take(TA, level, n, g[n])
            take(SY + level, level, n, dy(n + d))
            take(TY + level, level, n, dy(n))
        need = {2: 11, 1: 9, 0: NB}[level]
        g = {
            n: plus(
                times(c[F01], g[n]),
                times(c[F00], g[n + d]),
                times(c[C0 + level], dy(n)),
                times(c[CD + level], dy(n + d)),
            )
            for n in range(need)
        }
    return sums, g


def run(work, saved, coef_ref, acc_ref, start, finish, unroll=1):
    for h in range(2):
        cols = pl.ds(h * LANES, LANES)

        def step(r, accs):
            accs = list(accs)
            grads = [start(n, r, cols) for n in range(NB)]
            at = 0
            for b, sources in work:
                c = [coef_ref[b, i, :, cols][None] for i in range(COEFS)]
                dys = {}
                for ref, base in sources:
                    for j in range(NB):
                        if base + j < 23:
                            dys[base + j] = wide(ref[rows_of(b, j, r), cols])

                def p(level, n):
                    return wide(saved[3 * b + level if level else 0, rows_of(b, n, r), cols])

                sums, g = share(c, dys, p)
                for row in range(SUMS):
                    if sums[row] is not None:
                        accs[at + row] = accs[at + row] + (sums[row][0] + sums[row][1])
                at += SUMS
                for n in range(NB):
                    block = n if b == 0 else NB - 1 - n
                    grads[block] = plus(grads[block], g[n])
            for n in range(NB):
                finish(n, r, cols, grads[n].reshape(STEP, LANES))
            return tuple(accs)

        zero = jnp.zeros((STEP // 2, LANES), F32)
        accs = lax.fori_loop(0, BLOCK // STEP, step, (zero,) * (SUMS * len(work)), unroll=unroll)
        for i, (b, _) in enumerate(work):
            for row in range(SUMS):
                at = (b, pl.ds(row, 1), cols)
                acc_ref[at] = acc_ref[at] + jnp.sum(accs[i * SUMS + row], axis=0, keepdims=True)


def near_kernel(dy_hbm, first, fwd, rev, filters_hbm, mixing_hbm, acc_ref, part_ref, coef_ref, par_ref, saved, dy_ref, filters_ref, mixing_ref, sems):
    moves = [
        (filters_hbm, filters_ref),
        (mixing_hbm, mixing_ref),
        (dy_hbm, dy_ref),
        (first, saved.at[0]),
        (fwd, saved.at[pl.ds(1, LEVELS - 1)]),
        (rev, saved.at[pl.ds(LEVELS, LEVELS - 1)]),
    ]
    copies = [pltpu.make_async_copy(a, b, sems.at[i]) for i, (a, b) in enumerate(moves)]
    for copy in copies:
        copy.start()
    acc_ref[...] = jnp.zeros_like(acc_ref)
    for copy in copies[:2]:
        copy.wait()
    for b in range(2):
        f = [[filters_ref[b, i, pl.ds(j, 1), :] for j in range(2)] for i in range(2)]
        mix = [mixing_ref[i, pl.ds(b, 1), :] for i in range(LEVELS + 1)]
        c = [None] * COEFS
        c[F00], c[F01] = f[0]
        c[W0] = f[0][1] * mix[4] + f[1][1] * mix[3]
        c[W8] = f[0][0] * mix[4] + f[1][0] * mix[3]
        for level in range(3):
            c[C0 + level] = f[1][1] * mix[level]
            c[CD + level] = f[1][0] * mix[level]
        for i in range(COEFS):
            coef_ref[b, i] = jnp.broadcast_to(c[i], coef_ref.shape[2:])
        for i, value in enumerate([*f[0], *f[1], *mix]):
            par_ref[i, pl.ds(b, 1), :] = value
    for copy in copies[2:]:
        copy.wait()

    def keep(n, r, cols, value):
        part_ref[rows_of(0, n, r), cols] = value

    work = [(0, [(dy_ref, 0)]), (1, [(dy_ref, 0)])]
    run(work, saved, coef_ref, acc_ref, lambda n, r, cols: None, keep)


def pick_kernel(ids_ref, even_ref, odd_ref, cross_ref, turn_ref, left_ref, right_ref, send_ref):
    ids = ids_ref[0]
    core, detour, odd, place = ids % 2, ids // 2 % 2, ids // 4 % 2, ids // 8

    def copy(a, *to):
        def step(i, carry):
            rows = pl.ds(pl.multiple_of(i * BLOCK, BLOCK), BLOCK)
            value = a[rows, :]
            for b in to:
                b[rows, :] = value
            return carry

        lax.fori_loop(0, NB, step, 0)

    for side, to_ref in enumerate((left_ref, right_ref)):
        edge = place == side
        pl.when(edge & (detour == 0))(lambda to_ref=to_ref: copy(cross_ref, to_ref))
        pl.when(edge & (detour == 1))(lambda to_ref=to_ref: copy(turn_ref, to_ref))
        pl.when((place != side) & (odd != side))(lambda to_ref=to_ref: copy(even_ref, to_ref))
        pl.when((place != side) & (odd == side))(lambda to_ref=to_ref: copy(odd_ref, to_ref))
    pl.when(core == 0)(lambda: copy(right_ref, send_ref))
    pl.when(core == 1)(lambda: copy(left_ref, send_ref))


def far_kernel(ids_ref, swap_ref, right_ref, left_ref, saved, coef_ref, near_ref, part_ref, acc_ref, out_ref):
    core = ids_ref[0] % 2
    acc_ref[...] = near_ref[...]

    def start(n, r, cols):
        return part_ref[rows_of(0, n, r), cols].reshape(2, STEP // 2, LANES)

    def keep(n, r, cols, value):
        out_ref[rows_of(0, n, r), cols] = value

    for b in range(2):
        far = [[(right_ref, 2 * NB)], [(left_ref, 2 * NB)]]
        far[b] = [(swap_ref, NB)] + far[b]
        work = list(enumerate(far))
        pl.when(core == b)(lambda work=work: run(work, saved, coef_ref, acc_ref, start, keep, unroll=8))


def last_kernel(ids_ref, relay_ref, saved, par_ref, coef_ref, far_ref, part_ref, sums_ref, grad_ref, acc_ref, sum_ref):
    core = ids_ref[0] % 2
    acc_ref[...] = far_ref[...]
    sum_ref[...] = jnp.zeros_like(sum_ref)

    def start(n, r, cols):
        return part_ref[rows_of(0, n, r), cols].reshape(2, STEP // 2, LANES)

    def keep(n, r, cols, value):
        grad_ref[rows_of(0, n, r), cols] = value.astype(grad_ref.dtype)

    for b in range(2):
        work = [(b, [(relay_ref, NB)])]
        pl.when(core == 1 - b)(
            lambda work=work: run(work, saved, coef_ref, acc_ref, start, keep, unroll=8)
        )
    f = [[par_ref[2 * i + j] for j in range(2)] for i in range(2)]
    mix = [par_ref[4 + i] for i in range(LEVELS + 1)]
    acc = [acc_ref[:, i, :] for i in range(SUMS)]
    s, t = acc[SY : SY + LEVELS], acc[TY : TY + LEVELS]
    sums = [
        acc[SA] + mix[4] * s[3],
        acc[TA] + mix[4] * t[3],
        sum(mix[i] * s[i] for i in range(LEVELS)),
        sum(mix[i] * t[i] for i in range(LEVELS)),
        *(f[1][0] * s[i] + f[1][1] * t[i] for i in range(LEVELS)),
        f[0][0] * s[3] + f[0][1] * t[3],
    ]
    for b in range(2):
        for j, value in enumerate(sums):
            for h in range(2):
                at = 2 * (b * 9 + j) + h
                sum_ref[pl.ds(at, 1), :] = value[b : b + 1, h * LANES : (h + 1) * LANES]
    sent = sum_ref[...].astype(sums_ref.dtype)
    for copy in range(sums_ref.shape[0]):
        sums_ref[copy] = sent


def total_of(got_ref):
    total = got_ref[0].astype(F32)
    for i in range(1, got_ref.shape[0]):
        total = total + got_ref[i].astype(F32)
    return total


def fold_kernel(got_ref, sums_ref):
    total = total_of(got_ref).astype(sums_ref.dtype)
    for copy in range(sums_ref.shape[0]):
        sums_ref[copy] = total


def finish_kernel(factor, got_ref, grad_ref, filters_hbm, mixing_hbm, grad_hbm, filters_ref, mixing_ref, sems):
    moves = ((grad_ref, grad_hbm), (filters_ref, filters_hbm), (mixing_ref, mixing_hbm))
    copies = [pltpu.make_async_copy(a, b, sems.at[i]) for i, (a, b) in enumerate(moves)]
    copies[0].start()
    total = total_of(got_ref) * factor
    for b in range(2):
        for j in range(9):
            for h in range(2):
                row = total[2 * (b * 9 + j) + h : 2 * (b * 9 + j) + h + 1]
                cols = pl.ds(h * LANES, LANES)
                if j < 4:
                    filters_ref[b, j // 2, pl.ds(j % 2, 1), cols] = row
                else:
                    mixing_ref[j - 4, pl.ds(b, 1), cols] = row
    for copy in copies[1:]:
        copy.start()
    for copy in copies:
        copy.wait()


def call(kernel, name, outs, args, spaces, scratch=(), flops=0, spaces_out=None):
    space = {"s": pltpu.SMEM, "v": pltpu.VMEM, "h": pltpu.HBM, "a": pl.ANY}
    args = [pltpu.with_memory_space_constraint(a, pltpu.HBM) if k == "h" else a for a, k in zip(args, spaces)]
    return pl.pallas_call(
        kernel,
        out_shape=outs,
        in_specs=[pl.BlockSpec(memory_space=space[k]) for k in spaces],
        out_specs=tuple(pl.BlockSpec(memory_space=space[k]) for k in spaces_out or "v" * len(outs)),
        scratch_shapes=scratch,
        compiler_params=pltpu.CompilerParams(vmem_limit_bytes=8 * 1024 * 1024),
        cost_estimate=pl.CostEstimate(flops=flops, bytes_accessed=6_000_000, transcendentals=0),
        name=name,
    )(*args)


SEAM = ("zl",) + CTX


def routes():
    halves, zs, ys, cores = (lax.axis_size(axis) for axis in SEAM)

    def at(half, z, y, c):
        return ((half * zs + z) * ys + y) * cores + c

    spots = [(z, c) for z in range(zs) for c in range(cores)]
    next_to = [[(at(0, z, y, c), at(0, z, y + 1, c)) for z, c in spots for y in range(odd, ys - 1, 2)] for odd in range(2)]
    even, odd = [pairs + [(b, a) for a, b in pairs] for pairs in next_to]
    cross, hop, turn = [], [], []
    end = ys - 1
    for half in range(halves):
        for z, c in spots:
            if z + 1 == zs:
                continue
            last, first = at(half, z, end, c), at(half, z + 1, 0, c)
            if (half, c) != (0, 1):
                cross += [(last, first), (first, last)]
                continue
            for a, middle, b in ((last, at(half, z + 1, end, c), first), (first, at(half, z, 0, c), last)):
                hop.append((a, middle))
                turn.append((middle, b))
    return even, odd, cross, hop, turn


def body(level_input, saved_forward, saved_reverse, filters, mixing, cotangent):
    width = level_input.shape[2]
    rows = level_input.shape[1]
    ctx = lax.axis_size(CTX)
    core = lax.axis_index("core")
    dy = cotangent[0]
    mixing = jnp.swapaxes(mixing, 0, 1)
    acc = jax.ShapeDtypeStruct((2, ROWS, width), F32)
    part = jax.ShapeDtypeStruct((rows, width), F32)
    pair = [(0, 1), (1, 0)]
    even, odd, cross, hop, turn = routes()
    y = lax.axis_index("y")
    place = jnp.where(y == 0, 0, jnp.where(y == lax.axis_size("y") - 1, 1, 2))
    detour = jnp.where(lax.axis_index("zl") == 0, core, 0)
    ids = (core + 2 * detour + 4 * (y % 2) + 8 * place).astype(jnp.int32).reshape(1)
    ids, dy = lax.optimization_barrier((ids, dy))
    crossed = lax.ppermute(dy, SEAM, cross)
    hopped = lax.ppermute(dy, SEAM, hop)
    evens = lax.ppermute(dy, CTX, even)
    odds = lax.ppermute(dy, CTX, odd)
    swap = lax.ppermute(dy, "core", pair)
    acc_near, part_near, coef, par, saved = call(
        near_kernel,
        "near",
        (
            acc,
            part,
            jax.ShapeDtypeStruct((2, COEFS, STEP // 2, width), F32),
            jax.ShapeDtypeStruct((LEVELS + 5, 2, width), F32),
            jax.ShapeDtypeStruct((2 * LEVELS - 1, rows, width), dy.dtype),
        ),
        (dy, level_input[0], saved_forward[:, 0], saved_reverse[:, 0], filters, mixing),
        "hhhhhh",
        scratch=[
            pltpu.VMEM((rows, width), dy.dtype),
            pltpu.VMEM(filters.shape, F32),
            pltpu.VMEM(mixing.shape, F32),
            pltpu.SemaphoreType.DMA((6,)),
        ],
        flops=20_000_000,
    )
    hopped, acc_near = lax.optimization_barrier((hopped, acc_near))
    turned = lax.ppermute(hopped, SEAM, turn)
    crossed, turned, evens, odds = lax.optimization_barrier((crossed, turned, evens, odds))
    halo = jax.ShapeDtypeStruct(dy.shape, dy.dtype)
    left, right, send = call(pick_kernel, "pick", (halo,) * 3, (ids, evens, odds, crossed, turned), "svvvv")
    relay = lax.ppermute(send, "core", pair)
    acc_far, part_far = call(
        far_kernel,
        "far",
        (acc, part),
        (ids, swap, right, left, saved, coef, acc_near, part_near),
        "svvvvvvv",
        flops=20_000_000,
    )
    sums, grad = call(
        last_kernel,
        "last",
        (jax.ShapeDtypeStruct((8, SENT, LANES), F32), pltpu.VMEM((rows, width), jnp.bfloat16)),
        (ids, relay, saved, par, coef, acc_far, part_far),
        "svvvvvv",
        scratch=[
            pltpu.VMEM((2, ROWS, width), F32),
            pltpu.VMEM((SENT, LANES), F32),
        ],
        flops=20_000_000,
    )
    groups = (("x", "core"), ("y",), ("zl", "zh"))
    for i, axes in enumerate(groups):
        got = lax.all_to_all(sums, axes, 0, 0)
        if i + 1 < len(groups):
            (sums,) = call(fold_kernel, "fold", (jax.ShapeDtypeStruct(sums.shape, sums.dtype),), (got,), "v")
    count = level_input.shape[0] * lax.axis_size(DP) * rows * ctx
    grad_filters, grad_mixing, grad = call(
        lambda *refs: finish_kernel(1.0 / math.sqrt(count), *refs),
        "finish",
        (jax.ShapeDtypeStruct(filters.shape, F32), jax.ShapeDtypeStruct(mixing.shape, F32), jax.ShapeDtypeStruct(grad.shape, grad.dtype)),
        (got, grad),
        "vv",
        scratch=[
            pltpu.VMEM(filters.shape, F32),
            pltpu.VMEM(mixing.shape, F32),
            pltpu.SemaphoreType.DMA((3,)),
        ],
        spaces_out="aaa",
    )
    return grad[None], grad_filters, jnp.swapaxes(grad_mixing, 0, 1)


def solution(mesh):
    fine = Mesh(mesh.devices.reshape(4, 2, 4, 8, 2), DP + CTX)
    return jax.shard_map(
        body,
        mesh=fine,
        in_specs=(
            P(DP, CTX, None),
            P(None, DP, CTX, None),
            P(None, DP, CTX, None),
            P(),
            P(),
            P(DP, CTX, None),
        ),
        out_specs=(P(DP, CTX, None), P(), P()),
        check_vma=False,
    )
```

```python
import math

import jax
import jax.numpy as jnp
from jax import lax
from jax.experimental import pallas as pl
from jax.experimental.pallas import tpu as pltpu
from jax.sharding import Mesh
from jax.sharding import PartitionSpec as P

BLOCK = 128
NB = 8
LEVELS = 4
STEP = 16
LANES = 128
F32 = jnp.float32
DP = ("x", "zl")
CTX = ("zh", "y", "core")
SA, TA, SY, TY = 0, 1, 2, 6
SUMS = 10
SENT = 48
ROWS = 16
F00, F01, W0, W8, C0, CD = 0, 1, 2, 3, 4, 7
COEFS = 10


def rows_of(b, n, r):
    block = n if b == 0 else NB - 1 - n
    return pl.ds(pl.multiple_of(block * BLOCK + r * STEP, STEP), STEP)


def wide(value):
    return value.astype(F32).reshape(2, STEP // 2, LANES)


def times(c, v):
    return None if v is None else c * v


def plus(*terms):
    total = None
    for term in terms:
        if term is not None:
            total = term if total is None else total + term
    return total


def share(c, dys, p):
    dy = dys.get
    sums = [None] * SUMS

    def take(row, level, n, value):
        if value is not None:
            sums[row] = plus(sums[row], p(level, n) * value)

    g = {n: plus(times(c[W0], dy(n)), times(c[W8], dy(n + 8))) for n in range(15)}
    for n in range(NB):
        take(SY + 3, 3, n, dy(n + 8))
        take(TY + 3, 3, n, dy(n))
    for level in (2, 1, 0):
        d = 2**level
        for n in range(NB):
            take(SA, level, n, g[n + d])
            take(TA, level, n, g[n])
            take(SY + level, level, n, dy(n + d))
            take(TY + level, level, n, dy(n))
        need = {2: 11, 1: 9, 0: NB}[level]
        g = {
            n: plus(
                times(c[F01], g[n]),
                times(c[F00], g[n + d]),
                times(c[C0 + level], dy(n)),
                times(c[CD + level], dy(n + d)),
            )
            for n in range(need)
        }
    return sums, g


def run(work, saved, coef_ref, acc_ref, start, finish, unroll=1):
    for h in range(2):
        cols = pl.ds(h * LANES, LANES)

        def step(r, accs):
            accs = list(accs)
            grads = [start(n, r, cols) for n in range(NB)]
            at = 0
            for b, sources in work:
                c = [coef_ref[b, i, :, cols][None] for i in range(COEFS)]
                dys = {}
                for ref, base in sources:
                    for j in range(NB):
                        if base + j < 23:
                            dys[base + j] = wide(ref[rows_of(b, j, r), cols])

                def p(level, n):
                    return wide(saved[3 * b + level if level else 0, rows_of(b, n, r), cols])

                sums, g = share(c, dys, p)
                for row in range(SUMS):
                    if sums[row] is not None:
                        accs[at + row] = accs[at + row] + (sums[row][0] + sums[row][1])
                at += SUMS
                for n in range(NB):
                    block = n if b == 0 else NB - 1 - n
                    grads[block] = plus(grads[block], g[n])
            for n in range(NB):
                finish(n, r, cols, grads[n].reshape(STEP, LANES))
            return tuple(accs)

        zero = jnp.zeros((STEP // 2, LANES), F32)
        accs = lax.fori_loop(0, BLOCK // STEP, step, (zero,) * (SUMS * len(work)), unroll=unroll)
        for i, (b, _) in enumerate(work):
            for row in range(SUMS):
                at = (b, pl.ds(row, 1), cols)
                acc_ref[at] = acc_ref[at] + jnp.sum(accs[i * SUMS + row], axis=0, keepdims=True)


def near_kernel(dy_hbm, first, fwd, rev, filters_hbm, mixing_hbm, acc_ref, part_ref, coef_ref, par_ref, saved, dy_ref, filters_ref, mixing_ref, sems):
    moves = [
        (filters_hbm, filters_ref),
        (mixing_hbm, mixing_ref),
        (dy_hbm, dy_ref),
        (first, saved.at[0]),
        (fwd, saved.at[pl.ds(1, LEVELS - 1)]),
        (rev, saved.at[pl.ds(LEVELS, LEVELS - 1)]),
    ]
    copies = [pltpu.make_async_copy(a, b, sems.at[i]) for i, (a, b) in enumerate(moves)]
    for copy in copies:
        copy.start()
    acc_ref[...] = jnp.zeros_like(acc_ref)
    for copy in copies[:2]:
        copy.wait()
    for b in range(2):
        f = [[filters_ref[b, i, pl.ds(j, 1), :] for j in range(2)] for i in range(2)]
        mix = [mixing_ref[i, pl.ds(b, 1), :] for i in range(LEVELS + 1)]
        c = [None] * COEFS
        c[F00], c[F01] = f[0]
        c[W0] = f[0][1] * mix[4] + f[1][1] * mix[3]
        c[W8] = f[0][0] * mix[4] + f[1][0] * mix[3]
        for level in range(3):
            c[C0 + level] = f[1][1] * mix[level]
            c[CD + level] = f[1][0] * mix[level]
        for i in range(COEFS):
            coef_ref[b, i] = jnp.broadcast_to(c[i], coef_ref.shape[2:])
        for i, value in enumerate([*f[0], *f[1], *mix]):
            par_ref[i, pl.ds(b, 1), :] = value
    for copy in copies[2:]:
        copy.wait()

    def keep(n, r, cols, value):
        part_ref[rows_of(0, n, r), cols] = value

    work = [(0, [(dy_ref, 0)]), (1, [(dy_ref, 0)])]
    run(work, saved, coef_ref, acc_ref, lambda n, r, cols: None, keep)


def pick_kernel(ids_ref, even_ref, odd_ref, cross_ref, turn_ref, late_ref, send_ref):
    ids = ids_ref[0]
    core, detour, odd, edge = ids % 2, ids // 2 % 2, ids // 4 % 2, ids // 8

    def copy(a, *to):
        def step(i, carry):
            rows = pl.ds(pl.multiple_of(i * BLOCK, BLOCK), BLOCK)
            value = a[rows, :]
            for b in to:
                b[rows, :] = value
            return carry

        lax.fori_loop(0, NB, step, 0)

    pl.when((edge == 1) & (detour == 0))(lambda: copy(cross_ref, late_ref))
    pl.when((edge == 1) & (detour == 1))(lambda: copy(turn_ref, late_ref))
    pl.when(core == odd)(lambda: copy(even_ref, send_ref))
    pl.when(core != odd)(lambda: copy(late_ref, send_ref))


def far_kernel(ids_ref, swap_ref, even_ref, late_ref, saved, coef_ref, near_ref, part_ref, acc_ref, out_ref):
    core, odd = ids_ref[0] % 2, ids_ref[0] // 4 % 2
    acc_ref[...] = near_ref[...]

    def start(n, r, cols):
        return part_ref[rows_of(0, n, r), cols].reshape(2, STEP // 2, LANES)

    def keep(n, r, cols, value):
        out_ref[rows_of(0, n, r), cols] = value

    for b in range(2):
        for o in range(2):
            right, left = (late_ref, even_ref) if o else (even_ref, late_ref)
            far = [[(right, 2 * NB)], [(left, 2 * NB)]]
            far[b] = [(swap_ref, NB)] + far[b]
            work = list(enumerate(far))
            pl.when((core == b) & (odd == o))(
                lambda work=work: run(work, saved, coef_ref, acc_ref, start, keep, unroll=8)
            )


def last_kernel(ids_ref, relay_ref, saved, par_ref, coef_ref, far_ref, part_ref, sums_ref, grad_ref, acc_ref, sum_ref):
    core = ids_ref[0] % 2
    acc_ref[...] = far_ref[...]
    sum_ref[...] = jnp.zeros_like(sum_ref)

    def start(n, r, cols):
        return part_ref[rows_of(0, n, r), cols].reshape(2, STEP // 2, LANES)

    def keep(n, r, cols, value):
        grad_ref[rows_of(0, n, r), cols] = value.astype(grad_ref.dtype)

    for b in range(2):
        work = [(b, [(relay_ref, NB)])]
        pl.when(core == 1 - b)(
            lambda work=work: run(work, saved, coef_ref, acc_ref, start, keep, unroll=8)
        )
    f = [[par_ref[2 * i + j] for j in range(2)] for i in range(2)]
    mix = [par_ref[4 + i] for i in range(LEVELS + 1)]
    acc = [acc_ref[:, i, :] for i in range(SUMS)]
    s, t = acc[SY : SY + LEVELS], acc[TY : TY + LEVELS]
    sums = [
        acc[SA] + mix[4] * s[3],
        acc[TA] + mix[4] * t[3],
        sum(mix[i] * s[i] for i in range(LEVELS)),
        sum(mix[i] * t[i] for i in range(LEVELS)),
        *(f[1][0] * s[i] + f[1][1] * t[i] for i in range(LEVELS)),
        f[0][0] * s[3] + f[0][1] * t[3],
    ]
    for b in range(2):
        for j, value in enumerate(sums):
            for h in range(2):
                at = 2 * (b * 9 + j) + h
                sum_ref[pl.ds(at, 1), :] = value[b : b + 1, h * LANES : (h + 1) * LANES]
    sent = sum_ref[...].astype(sums_ref.dtype)
    for copy in range(sums_ref.shape[0]):
        sums_ref[copy] = sent


def total_of(got_ref):
    total = got_ref[0].astype(F32)
    for i in range(1, got_ref.shape[0]):
        total = total + got_ref[i].astype(F32)
    return total


def fold_kernel(got_ref, sums_ref):
    total = total_of(got_ref).astype(sums_ref.dtype)
    for copy in range(sums_ref.shape[0]):
        sums_ref[copy] = total


def finish_kernel(factor, got_ref, grad_ref, filters_hbm, mixing_hbm, grad_hbm, filters_ref, mixing_ref, sems):
    moves = ((grad_ref, grad_hbm), (filters_ref, filters_hbm), (mixing_ref, mixing_hbm))
    copies = [pltpu.make_async_copy(a, b, sems.at[i]) for i, (a, b) in enumerate(moves)]
    copies[0].start()
    total = total_of(got_ref) * factor
    for b in range(2):
        for j in range(9):
            for h in range(2):
                row = total[2 * (b * 9 + j) + h : 2 * (b * 9 + j) + h + 1]
                cols = pl.ds(h * LANES, LANES)
                if j < 4:
                    filters_ref[b, j // 2, pl.ds(j % 2, 1), cols] = row
                else:
                    mixing_ref[j - 4, pl.ds(b, 1), cols] = row
    for copy in copies[1:]:
        copy.start()
    for copy in copies:
        copy.wait()


def call(kernel, name, outs, args, spaces, scratch=(), flops=0, spaces_out=None, aliases={}):
    space = {"s": pltpu.SMEM, "v": pltpu.VMEM, "h": pltpu.HBM, "a": pl.ANY}
    args = [pltpu.with_memory_space_constraint(a, pltpu.HBM) if k == "h" else a for a, k in zip(args, spaces)]
    return pl.pallas_call(
        kernel,
        out_shape=outs,
        in_specs=[pl.BlockSpec(memory_space=space[k]) for k in spaces],
        out_specs=tuple(pl.BlockSpec(memory_space=space[k]) for k in spaces_out or "v" * len(outs)),
        scratch_shapes=scratch,
        input_output_aliases=aliases,
        compiler_params=pltpu.CompilerParams(vmem_limit_bytes=8 * 1024 * 1024),
        cost_estimate=pl.CostEstimate(flops=flops, bytes_accessed=6_000_000, transcendentals=0),
        name=name,
    )(*args)


SEAM = ("zl",) + CTX


def routes():
    halves, zs, ys, cores = (lax.axis_size(axis) for axis in SEAM)

    def at(half, z, y, c):
        return ((half * zs + z) * ys + y) * cores + c

    spots = [(z, c) for z in range(zs) for c in range(cores)]
    next_to = [[(at(0, z, y, c), at(0, z, y + 1, c)) for z, c in spots for y in range(odd, ys - 1, 2)] for odd in range(2)]
    even, odd = [pairs + [(b, a) for a, b in pairs] for pairs in next_to]
    cross, hop, turn = [], [], []
    end = ys - 1
    for half in range(halves):
        for z, c in spots:
            if z + 1 == zs:
                continue
            last, first = at(half, z, end, c), at(half, z + 1, 0, c)
            if (half, c) != (0, 1):
                cross += [(last, first), (first, last)]
                continue
            for a, middle, b in ((last, at(half, z + 1, end, c), first), (first, at(half, z, 0, c), last)):
                hop.append((a, middle))
                turn.append((middle, b))
    return even, odd, cross, hop, turn


def body(level_input, saved_forward, saved_reverse, filters, mixing, cotangent):
    width = level_input.shape[2]
    rows = level_input.shape[1]
    ctx = lax.axis_size(CTX)
    core = lax.axis_index("core")
    dy = cotangent[0]
    mixing = jnp.swapaxes(mixing, 0, 1)
    acc = jax.ShapeDtypeStruct((2, ROWS, width), F32)
    part = jax.ShapeDtypeStruct((rows, width), F32)
    pair = [(0, 1), (1, 0)]
    even, odd, cross, hop, turn = routes()
    y = lax.axis_index("y")
    edge = jnp.where((y == 0) | (y == lax.axis_size("y") - 1), 1, 0)
    detour = jnp.where(lax.axis_index("zl") == 0, core, 0)
    ids = (core + 2 * detour + 4 * (y % 2) + 8 * edge).astype(jnp.int32).reshape(1)
    ids, dy = lax.optimization_barrier((ids, dy))
    crossed = lax.ppermute(dy, SEAM, cross)
    hopped = lax.ppermute(dy, SEAM, hop)
    evens = lax.ppermute(dy, CTX, even)
    odds = lax.ppermute(dy, CTX, odd)
    swap = lax.ppermute(dy, "core", pair)
    acc_near, part_near, coef, par, saved = call(
        near_kernel,
        "near",
        (
            acc,
            part,
            jax.ShapeDtypeStruct((2, COEFS, STEP // 2, width), F32),
            jax.ShapeDtypeStruct((LEVELS + 5, 2, width), F32),
            jax.ShapeDtypeStruct((2 * LEVELS - 1, rows, width), dy.dtype),
        ),
        (dy, level_input[0], saved_forward[:, 0], saved_reverse[:, 0], filters, mixing),
        "hhhhhh",
        scratch=[
            pltpu.VMEM((rows, width), dy.dtype),
            pltpu.VMEM(filters.shape, F32),
            pltpu.VMEM(mixing.shape, F32),
            pltpu.SemaphoreType.DMA((6,)),
        ],
        flops=20_000_000,
    )
    hopped, acc_near = lax.optimization_barrier((hopped, acc_near))
    turned = lax.ppermute(hopped, SEAM, turn)
    crossed, turned, evens, odds = lax.optimization_barrier((crossed, turned, evens, odds))
    halo = jax.ShapeDtypeStruct(dy.shape, dy.dtype)
    late, send = call(pick_kernel, "pick", (halo,) * 2, (ids, evens, odds, crossed, turned), "svvvv", aliases={2: 0})
    relay = lax.ppermute(send, "core", pair)
    acc_far, part_far = call(
        far_kernel,
        "far",
        (acc, part),
        (ids, swap, evens, late, saved, coef, acc_near, part_near),
        "svvvvvvv",
        flops=20_000_000,
    )
    sums, grad = call(
        last_kernel,
        "last",
        (jax.ShapeDtypeStruct((8, SENT, LANES), dy.dtype), pltpu.VMEM((rows, width), jnp.bfloat16)),
        (ids, relay, saved, par, coef, acc_far, part_far),
        "svvvvvv",
        scratch=[
            pltpu.VMEM((2, ROWS, width), F32),
            pltpu.VMEM((SENT, LANES), F32),
        ],
        flops=20_000_000,
    )
    groups = (("x", "core"), ("y",), ("zl", "zh"))
    for i, axes in enumerate(groups):
        got = lax.all_to_all(sums, axes, 0, 0)
        if i + 1 < len(groups):
            (sums,) = call(fold_kernel, "fold", (jax.ShapeDtypeStruct(sums.shape, sums.dtype),), (got,), "v")
    count = level_input.shape[0] * lax.axis_size(DP) * rows * ctx
    grad_filters, grad_mixing, grad = call(
        lambda *refs: finish_kernel(1.0 / math.sqrt(count), *refs),
        "finish",
        (jax.ShapeDtypeStruct(filters.shape, F32), jax.ShapeDtypeStruct(mixing.shape, F32), jax.ShapeDtypeStruct(grad.shape, grad.dtype)),
        (got, grad),
        "vv",
        scratch=[
            pltpu.VMEM(filters.shape, F32),
            pltpu.VMEM(mixing.shape, F32),
            pltpu.SemaphoreType.DMA((3,)),
        ],
        spaces_out="aaa",
    )
    return grad[None], grad_filters, jnp.swapaxes(grad_mixing, 0, 1)


def solution(mesh):
    fine = Mesh(mesh.devices.reshape(4, 2, 4, 8, 2), DP + CTX)
    return jax.shard_map(
        body,
        mesh=fine,
        in_specs=(
            P(DP, CTX, None),
            P(None, DP, CTX, None),
            P(None, DP, CTX, None),
            P(),
            P(),
            P(DP, CTX, None),
        ),
        out_specs=(P(DP, CTX, None), P(), P()),
        check_vma=False,
    )
```
